256 devices in a mesh: dp: 4 (over y), ctx: 64 (over x, z, core).
Axes of the slice: x: 4, y: 4, z: 8, core: 2. Of those that a mesh axis runs over, the one named last changes fastest.
Arguments:
- mamba_input: bfloat16 [32768, 4096], P(('dp', 'ctx')), parts along dimension 0, may hold values from -6 to 6
- gate_branch: bfloat16 [32768, 4096], P(('dp', 'ctx')), parts along dimension 0, may hold values from -6 to 6
- step_size: bfloat16 [32768, 4096], P(('dp', 'ctx')), parts along dimension 0, may hold values from 0.5 to 24576
- decay_rates: float32 [16384, 16], P('dp'), parts along dimension 0, may hold values from -0.07 to 0
- input_map: bfloat16 [32768, 16], P(('dp', 'ctx')), parts along dimension 0, may hold values from -3 to 3
- output_map: bfloat16 [32768, 16], P(('dp', 'ctx')), parts along dimension 0, may hold values from -3 to 3
- mixing_weight: bfloat16 [4, 4096], replicated, may hold values from -3 to 3
- mixing_bias: bfloat16 [4096], replicated, may hold values from -3 to 3
- skip_gain: float32 [4096], replicated, may hold values from 0.5 to 1.5
- segments: int32 [32768], P('dp'), parts along dimension 0, may hold values from 0 to 3, never falling along the last dimension, each value on 1 to 6144 neighbouring positions
- query_rows: bfloat16 [32768, 2048], P(('dp', 'ctx')), parts along dimension 0, may hold values from -7 to 7
- key_rows: bfloat16 [32768, 512], P(('dp', 'ctx')), parts along dimension 0, may hold values from -4 to 4
- value_rows: bfloat16 [32768, 512], P(('dp', 'ctx')), parts along dimension 0, may hold values from -6 to 6
Outputs:
- mamba_output: bfloat16 [32768, 4096], P(('dp', 'ctx')), parts along dimension 0
- attention_output: bfloat16 [32768, 2048], P(('dp', 'ctx')), parts along dimension 0
The draws below stay inside these ranges and needn't reach their ends.
There are 4 independent parts, one for each index of `dp`. The reference program is written for one: setup_inputs(seed, part) draws one part's arguments, and reference() takes and returns one part's arrays. A program takes and returns all parts, laid end to end along the dimension named above; an argument that names none is the same for every part. Nothing has to cross between parts.
Inputs may be any that keep to these rules, and one draw needn't show every extreme that they name: `segments`: each of the 4 documents is one run of consecutive positions, numbered in order; the longest has exactly 6144 positions.
All inputs are finite; a program needn't handle non-finite values.
Results may differ from the reference program's by a relative error of at most 0.005.
Values may be sent and summed in bfloat16 or wider, within the bound.
A program may use at most 128 MiB of HBM per device.

```python
import math
import jax
import jax.numpy as jnp
import numpy as np
from jax import lax

INNER_CHANNELS = 4096
NS = 16
KW = 4
HQ = 16
KVH = 4
HD = 128
DOCS = 4
SEQUENCE_LENGTH = 8192


def channel_memory(base_key, slow_share, slow_low, slow_high, fast_low, fast_high):
    pick_key, slow_key, fast_key = jax.random.split(jax.random.fold_in(base_key, 101), 3)
    slow_mask = jax.random.bernoulli(pick_key, slow_share, (INNER_CHANNELS,))
    slow_memory = jnp.exp(jax.random.uniform(slow_key, (INNER_CHANNELS,), minval=math.log(slow_low), maxval=math.log(slow_high)))
    fast_memory = jnp.exp(jax.random.uniform(fast_key, (INNER_CHANNELS,), minval=math.log(fast_low), maxval=math.log(fast_high)))
    return jnp.where(slow_mask, slow_memory, fast_memory)


def draw_decay_rates(key, part):
    recurrent_state = channel_memory(key, 0.5, 1.0 * SEQUENCE_LENGTH, 4.0 * SEQUENCE_LENGTH, 30.0, max(60.0, SEQUENCE_LENGTH / 4.0))
    key = jax.random.fold_in(key, 5)
    spread = jnp.exp(jax.random.uniform(key, (INNER_CHANNELS, NS), minval=math.log(0.5), maxval=math.log(2.0)))
    return (-spread / recurrent_state[:, None]).astype(jnp.float32)


def draw_step_size(key, part):
    recurrent_state = channel_memory(key, 0.5, 1.0 * SEQUENCE_LENGTH, 4.0 * SEQUENCE_LENGTH, 30.0, max(60.0, SEQUENCE_LENGTH / 4.0))
    key = jax.random.fold_in(key, 7)
    jitter_random_key, spike_random_key, magnitude_key = jax.random.split(key, 3)
    baseline_rows = jnp.exp(jax.random.uniform(jitter_random_key, (SEQUENCE_LENGTH, INNER_CHANNELS), minval=math.log(0.5), maxval=math.log(2.0)))
    spike_row_values = jax.random.randint(spike_random_key, (4,), 0, SEQUENCE_LENGTH)
    spike_selected = jnp.any(jnp.arange(SEQUENCE_LENGTH)[:, None] == spike_row_values[None, :], axis=1)
    spike_magnitude = jax.random.uniform(magnitude_key, (INNER_CHANNELS,), minval=0.25, maxval=0.35)
    return jnp.where(spike_selected[:, None], spike_magnitude[None, :] * recurrent_state[None, :], baseline_rows).astype(jnp.bfloat16)


def draw_key_rows(key, part):
    key = jax.random.fold_in(key, 11)
    values = jnp.clip(jax.random.normal(key, (SEQUENCE_LENGTH, KVH * HD)), -4.0, 4.0)
    return values.astype(jnp.bfloat16)


def draw_query_rows(key, part):
    key = jax.random.fold_in(key, 13)
    values = jnp.clip(jax.random.normal(key, (SEQUENCE_LENGTH, HQ * HD)), -4.0, 4.0)
    return values.astype(jnp.bfloat16)


def block_levels(own_key, shape, cuts, least, largest):
    factor_of = 1.0
    for axis_at, parts in cuts:
        steps = jax.random.uniform(jax.random.fold_in(jax.random.fold_in(own_key, 6), axis_at), (parts,), jnp.float32, least / len(cuts), largest / len(cuts))
        factor_of = factor_of * jnp.repeat(jnp.exp(steps), shape[axis_at] // parts).reshape((-1,) + (1,) * (len(shape) - 1 - axis_at))
    return factor_of


def split_up(count, total, reach, slope):
    loads = [(1 << 20) // math.isqrt(standing ** slope) + 1 for standing in range(2, count + 1)]
    spare, given = total - reach - (count - 1), [1] * (count - 1)
    while spare > 0:
        free = [i for i in range(count - 1) if given[i] < reach]
        pool, remaining = sum([loads[i] for i in free]), spare
        for i in free:
            more = min(reach - given[i], max(1, remaining * loads[i] // pool), spare)
            given[i] = given[i] + more
            spare = spare - more
    return np.array([reach] + given)


def ragged_sizes(rng, number_of, total, bound, lean):
    if number_of == 2:
        one = jax.random.randint(rng, (), max(1, total - bound), min(bound, total - 1) + 1)
        return jnp.stack([one, total - one])
    lengths = jnp.asarray(split_up(number_of, total, bound, lean), jnp.int32)
    couples = (number_of - 1) // 2
    giver, sink = lengths[1:1 + 2 * couples:2], lengths[2:2 + 2 * couples:2]
    room = jnp.minimum(giver - 1, bound - sink)
    passed = jax.random.randint(jax.random.fold_in(rng, 1), (couples,), 0, 1 << 20) % (room + 1)
    lengths = lengths.at[1:1 + 2 * couples:2].set(giver - passed).at[2:2 + 2 * couples:2].set(sink + passed)
    return lengths[jax.random.permutation(jax.random.fold_in(rng, 2), number_of)]


def scatter_about(key, shape, scale, most, cuts=(), held_as=jnp.bfloat16):
    entries = jax.random.normal(key, shape, jnp.float32) * scale
    if len(cuts) > 0:
        entries = block_levels(key, shape, cuts, -0.22, 0.18) * entries
    return jnp.clip(entries, min=-most, max=most).astype(held_as)


def setup_inputs(seed: int = 0, part: int = 0) -> dict:
    streams_of = jax.random.split(jax.random.key(seed), 14)
    part_keys = jax.random.split(jax.random.fold_in(streams_of[13], part), 14)
    mamba_input = scatter_about(part_keys[0], (SEQUENCE_LENGTH, INNER_CHANNELS), 1.0, 6.0, ((0, 64),))
    gate_branch = scatter_about(part_keys[1], (SEQUENCE_LENGTH, INNER_CHANNELS), 1.0, 6.0, ((0, 64),))
    step_size = draw_step_size(jax.random.fold_in(jax.random.fold_in(streams_of[13], part), 71), part)
    decay_rates = draw_decay_rates(jax.random.fold_in(jax.random.fold_in(streams_of[13], part), 71), part)
    input_map = scatter_about(part_keys[4], (SEQUENCE_LENGTH, NS), 0.5, 3.0, ((0, 64),))
    output_map = scatter_about(part_keys[5], (SEQUENCE_LENGTH, NS), 0.5, 3.0, ((0, 64),))
    mixing_weight = scatter_about(streams_of[6], (KW, INNER_CHANNELS), KW ** -0.5, 3.0)
    mixing_bias = scatter_about(streams_of[7], (INNER_CHANNELS,), 0.5, 3.0)
    skip_gain = jnp.clip(jax.random.uniform(streams_of[8], (INNER_CHANNELS,), jnp.float32, 0.5, 1.5), 0.5, 1.5)
    segments = jnp.searchsorted(jnp.cumsum(ragged_sizes(part_keys[9], DOCS, SEQUENCE_LENGTH, 3 * SEQUENCE_LENGTH // 4, 0)), jnp.arange(SEQUENCE_LENGTH), side="right").astype(jnp.int32)
    query_rows = draw_query_rows(jax.random.fold_in(jax.random.fold_in(streams_of[13], part), 71), part)
    key_rows = draw_key_rows(jax.random.fold_in(jax.random.fold_in(streams_of[13], part), 71), part)
    value_rows = scatter_about(part_keys[12], (SEQUENCE_LENGTH, KVH * HD), 1.0, 6.0, ((0, 64),))
    return dict(mamba_input=mamba_input, gate_branch=gate_branch, step_size=step_size, decay_rates=decay_rates, input_map=input_map, output_map=output_map, mixing_weight=mixing_weight, mixing_bias=mixing_bias, skip_gain=skip_gain, segments=segments, query_rows=query_rows, key_rows=key_rows, value_rows=value_rows)


def causal_mixing(extended, extended_ids, mixing_weight, mixing_bias):
    local_rows = extended.shape[0] - (KW - 1)
    here_ids = extended_ids[KW - 1:]
    summed = mixing_bias.astype(jnp.float32)[None, :] + mixing_weight[KW - 1].astype(jnp.float32)[None, :] * extended[KW - 1:].astype(jnp.float32)
    for delay in range(1, KW):
        earlier = extended[KW - 1 - delay:KW - 1 - delay + local_rows].astype(jnp.float32)
        allowed = (extended_ids[KW - 1 - delay:KW - 1 - delay + local_rows] == here_ids).astype(jnp.float32)[:, None]
        summed = summed + mixing_weight[KW - 1 - delay].astype(jnp.float32)[None, :] * earlier * allowed
    return jax.nn.silu(summed).astype(jnp.bfloat16)

def decay_terms(step_row, decay_rates, fresh):
    exponent = step_row.astype(jnp.float32)[:, None] * decay_rates
    factor = jnp.where(fresh > 0, jnp.float32(0.0), jnp.exp(exponent))
    weight = jnp.where(fresh > 0, jnp.float32(1.0), jnp.sqrt(-jnp.expm1(2.0 * exponent)))
    return (factor, weight)

def advance(carried, inputs, decay_rates):
    drive, step_row, in_row, out_row, fresh = inputs
    factor, weight = decay_terms(step_row, decay_rates, fresh)
    carried = factor * carried + weight * (in_row.astype(jnp.float32)[None, :] * drive.astype(jnp.float32)[:, None])
    return (carried, lax.optimization_barrier(jnp.sum(carried * out_row.astype(jnp.float32)[None, :], axis=1)))

def attend_block(block_q, block_pos, keys_all, values_all, segments):
    score_scale = block_q.shape[1] ** (-0.5)
    scores = lax.dot_general(block_q, keys_all, (((1,), (1,)), ((), ())), preferred_element_type=jnp.float32) * score_scale
    key_pos = jnp.arange(keys_all.shape[0], dtype=jnp.int32)
    query_ids = jnp.take(segments, block_pos)
    allowed = (key_pos[None, :] <= block_pos[:, None]) & (segments[None, :] == query_ids[:, None])
    masked = jnp.where(allowed, scores, jnp.float32(-1e+30))
    row_max = lax.optimization_barrier(jnp.max(masked, axis=1, keepdims=True))
    exp_terms = jnp.where(allowed, jnp.exp(masked - row_max), jnp.float32(0.0))
    row_total = lax.optimization_barrier(jnp.sum(exp_terms, axis=1, keepdims=True))
    probs = (exp_terms / row_total).astype(jnp.bfloat16)
    return jnp.dot(probs, values_all, preferred_element_type=jnp.float32).astype(jnp.bfloat16)

def reference(mamba_input, gate_branch, step_size, decay_rates, input_map, output_map, mixing_weight, mixing_bias, skip_gain, segments, query_rows, key_rows, value_rows):
    seq_len = mamba_input.shape[0]
    extended = jnp.concatenate([jnp.zeros((KW - 1, INNER_CHANNELS), jnp.bfloat16), mamba_input], axis=0)
    extended_ids = jnp.concatenate([jnp.full((KW - 1,), -1, jnp.int32), segments])
    conved = causal_mixing(extended, extended_ids, mixing_weight, mixing_bias)
    previous = jnp.concatenate([jnp.full((1,), -1, jnp.int32), segments[:-1]])
    fresh = ((segments != previous) & (previous >= 0)).astype(jnp.int32)

    def scan_step(carried, inputs):
        return advance(carried, inputs, decay_rates)
    _, readout = lax.scan(scan_step, jnp.zeros((INNER_CHANNELS, NS), jnp.float32), (conved, step_size, input_map, output_map, fresh))
    mamba_output = ((readout + skip_gain[None, :] * conved.astype(jnp.float32)) * jax.nn.silu(gate_branch.astype(jnp.float32))).astype(jnp.bfloat16)
    span = min(512, seq_len)
    queries = query_rows.reshape(seq_len, HQ, HD)
    keys_split = key_rows.reshape(seq_len, KVH, HD)
    values_split = value_rows.reshape(seq_len, KVH, HD)
    positions = jnp.arange(seq_len, dtype=jnp.int32).reshape(seq_len // span, span)

    def per_head(head):
        group = head // (HQ // KVH)
        head_q = lax.dynamic_index_in_dim(queries, head, 1, keepdims=False).reshape(seq_len // span, span, HD)
        head_k = lax.dynamic_index_in_dim(keys_split, group, 1, keepdims=False)
        head_v = lax.dynamic_index_in_dim(values_split, group, 1, keepdims=False)

        def one_block(item):
            return attend_block(item[0], item[1], head_k, head_v, segments)
        return lax.map(one_block, (head_q, positions))
    result = lax.map(per_head, jnp.arange(HQ, dtype=jnp.int32))
    attention_output = result.reshape(HQ, seq_len, HD).transpose(1, 0, 2).reshape(seq_len, HQ * HD)
    return (mamba_output, attention_output)
```

```python
import functools

import jax
import jax.numpy as jnp
from jax import lax
from jax.experimental import pallas as pl
from jax.experimental.pallas import tpu as pltpu
from jax.sharding import PartitionSpec as P

F32 = jnp.float32
BF16 = jnp.bfloat16
MESH = pl.DeviceIdType.MESH
LOG2E = 1.4426950408889634
LN2 = 0.6931471805599453

ROWS = 128
CH = 4096
NS = 16
PLANES = 4
RING = 16
ZN = 8
HD = 128
GROUP = 4
STEPS = 16
HUGE = 3e38
MASKED = -1e30
OWN = CH // RING
SCALE = LOG2E / HD**0.5
ROW_CONTRACT = (((0,), (0,)), ((), ()))
LANE_CONTRACT = (((1,), (1,)), ((), ()))


def iota(shape, dim):
    return lax.broadcasted_iota(jnp.int32, shape, dim)


def silu(v):
    return v / (1.0 + jnp.exp(-v))


def kernel(
    x_hbm, gate_hbm, step_hbm, decay_ref, in_ref, out_map_ref, taps_ref, bias_ref, skip_ref, seg_ref,
    q_hbm, k_hbm, v_hbm,
    mixed_hbm, attended_hbm,
    xv, gv, sv, halo, u_ref, s_ref, cum_ref, gs_ref, y_ref, ends_ref, rates_ref, rates_t, bb_ref, cc_ref,
    masks_ref, kv, q_in, q_aug, o_buf, m_out, totals, plane_in, plane_total, across_in, spread, entering,
    own_prefix,
    load_sem, halo_sem, qkv_send, qkv_recv, fwd_send, fwd_recv, bwd_send, bwd_recv, sib_send, sib_recv,
    tot_send, tot_recv, acr_send, acr_recv, spr_send, spr_recv, o_send, o_recv, own_sem, store_sem,
):
    dp = lax.axis_index("dp")
    me = lax.axis_index("ctx")
    plane = me // RING
    r = me % RING
    z = r // 2
    core = r % 2

    def at(p, rr):
        return (dp, p * RING + rr)

    def remote(src, dst, send, recv, target):
        return pltpu.make_async_remote_copy(
            src_ref=src, dst_ref=dst, send_sem=send, recv_sem=recv, device_id=target, device_id_type=MESH
        )

    loads = [
        pltpu.make_async_copy(x_hbm, xv, load_sem.at[0]),
        pltpu.make_async_copy(step_hbm, sv, load_sem.at[1]),
        pltpu.make_async_copy(gate_hbm, gv, load_sem.at[2]),
    ]
    for load in loads:
        load.start()

    barrier = pltpu.get_barrier_semaphore()

    @pl.loop(1, RING)
    def _(j):
        pl.semaphore_signal(barrier, inc=1, device_id=at(plane, (r + j) % RING), device_id_type=MESH)

    @pl.loop(1, PLANES)
    def _(j):
        pl.semaphore_signal(barrier, inc=1, device_id=at((plane + j) % PLANES, r), device_id_type=MESH)

    count = PLANES * RING
    pl.semaphore_signal(barrier, inc=1, device_id=(dp, (me + 1) % count), device_id_type=MESH)
    pl.semaphore_signal(barrier, inc=1, device_id=(dp, (me + count - 1) % count), device_id_type=MESH)
    pl.semaphore_wait(barrier, RING - 1 + PLANES - 1 + 2)

    halo_copy = remote(
        x_hbm.at[pl.ds(ROWS - 16, 16), :], halo, halo_sem.at[0], halo_sem.at[1], (dp, (me + 1) % count)
    )
    halo_copy.start()

    def qkv_parts(p):
        return [
            (k_hbm.at[:, pl.ds(pl.multiple_of(p * HD, HD), HD)], kv.at[plane, r, :, pl.ds(HD, HD)]),
            (v_hbm.at[:, pl.ds(pl.multiple_of(p * HD, HD), HD)], kv.at[plane, r, :, pl.ds(2 * HD, HD)]),
            (q_hbm.at[:, pl.ds(pl.multiple_of(p * GROUP * HD, HD), GROUP * HD)], q_in.at[plane]),
        ]

    def qkv_copies(o, parts=(0, 1, 2)):
        p = (plane + o) % PLANES
        pairs = qkv_parts(p)
        return [
            remote(pairs[i][0], pairs[i][1], qkv_send.at[o, i], qkv_recv.at[o, i], at(p, r)) for i in parts
        ]

    for parts in ((0, 1), (2,)):
        for o in range(1, PLANES):
            for copy in qkv_copies(o, parts):
                copy.start()
    own_qkv = [pltpu.make_async_copy(s, d, own_sem.at[i]) for i, (s, d) in enumerate(qkv_parts(plane))]
    for copy in own_qkv:
        copy.start()

    p_ids, t_ids = iota((ROWS, ROWS), 0), iota((ROWS, ROWS), 1)
    perm = (t_ids == (p_ids % 8) * STEPS + p_ids // 8).astype(F32)
    perm_b = perm.astype(BF16)
    ones = jnp.ones((ROWS, ROWS), BF16)

    seg = seg_ref[...].astype(F32)
    block_ids = iota((PLANES * RING, ROWS), 0)

    def seg_row(b):
        return jnp.sum(jnp.where(block_ids == b, seg, 0.0), axis=0, keepdims=True)

    here = jnp.broadcast_to(seg_row(me), (8, ROWS))
    before = jnp.broadcast_to(jnp.where(me > 0, seg_row(me - 1), -1.0), (8, ROWS))
    lane8 = iota((8, ROWS), 1)
    for d in range(1, 4):
        ids = jnp.where(lane8 >= d, pltpu.roll(here, d, 1), pltpu.roll(before, d, 1))
        same = (ids == here).astype(F32)
        masks_ref[d] = jnp.dot((perm * same[0:1]).astype(BF16), ones, preferred_element_type=F32)
        if d == 1:
            fresh = ((ids != here) & (ids >= 0.0)).astype(F32)
            masks_ref[0] = jnp.dot((perm * fresh[0:1]).astype(BF16), ones, preferred_element_type=F32)

    repeat = (iota((NS, NS * 128), 0) == iota((NS, NS * 128), 1) // 128).astype(BF16)
    for src, dst in ((in_ref, bb_ref), (out_map_ref, cc_ref)):
        ordered = jnp.dot(perm_b, src[...], preferred_element_type=F32).astype(BF16)
        dst[...] = jnp.dot(ordered, repeat, preferred_element_type=F32)

    @pl.loop(0, CH // 128)
    def _(cb):
        lanes = pl.ds(pl.multiple_of(cb * 128, 128), 128)
        rates = (jnp.minimum(decay_ref[lanes, :], -1e-30) * LOG2E).T
        rates_t[:, lanes] = rates
        for n in range(NS):
            rates_ref[n, :, lanes] = jnp.broadcast_to(rates[n : n + 1], (8, 128))

    unit = (iota((16, HD), 0) == iota((16, HD), 1)).astype(BF16)
    doc_ids = iota((16, ROWS), 0).astype(F32)

    @pl.loop(0, PLANES * RING // 8)
    def _(g):
        rows = seg_ref[pl.ds(pl.multiple_of(g * 8, 8), 8), :].astype(F32)
        for i in range(8):
            hot = (doc_ids == rows[i : i + 1]).astype(BF16)
            cols = lax.dot_general(hot, unit, ROW_CONTRACT, preferred_element_type=F32)
            kv[g // 2, (g % 2) * 8 + i, :, pl.ds(0, HD)] = cols.astype(BF16)

    for p in range(PLANES):
        ids = seg_row(p * RING + r)
        cold = jnp.where((doc_ids != ids) & (doc_ids < 4.0), MASKED, 0.0).astype(BF16)
        cols = lax.dot_general(cold, unit, ROW_CONTRACT, preferred_element_type=F32).astype(BF16)
        for h in range(GROUP):
            q_aug[p, pl.ds(h * ROWS, ROWS), pl.ds(0, HD)] = cols

    for load in loads:
        load.wait()
    halo_copy.wait()

    W = 256

    @pl.loop(0, CH // W)
    def _(b):
        lanes = pl.ds(pl.multiple_of(b * W, W), W)
        xp = jnp.dot(perm_b, xv[:, lanes], preferred_element_type=F32)
        sp = jnp.dot(perm_b, sv[:, lanes], preferred_element_type=F32)
        gp = jnp.dot(perm_b, gv[:, lanes], preferred_element_type=F32)
        edge = halo[:, lanes].astype(F32)
        first = iota((8, W), 0) == 0
        lead = []
        for d in (3, 2, 1):
            rolled = pltpu.roll(xp[(STEPS - d) * 8 : (STEPS - d + 1) * 8], 1, 0)
            lead.append(jnp.where(first, edge[16 - d : 17 - d], rolled))
        extended = jnp.concatenate(lead + [xp], axis=0)
        taps = taps_ref[:, lanes].astype(F32)
        summed = bias_ref[:, lanes].astype(F32) + taps[3:4] * xp
        for d in range(1, 4):
            allowed = jnp.concatenate([masks_ref[d]] * (W // 128), axis=1)
            earlier = extended[(3 - d) * 8 : (3 - d) * 8 + ROWS]
            summed = summed + taps[3 - d : 4 - d] * earlier * allowed
        u_ref[:, lanes] = silu(summed).astype(BF16).astype(F32)
        fresh = jnp.concatenate([masks_ref[0]] * (W // 128), axis=1)
        steps = jnp.where(fresh > 0.0, HUGE, sp)
        s_ref[:, lanes] = steps
        running = steps[0:8]
        cum_ref[pl.ds(0, 8), lanes] = running
        for i in range(1, STEPS):
            running = running + steps[i * 8 : i * 8 + 8]
            cum_ref[pl.ds(i * 8, 8), lanes] = running
        gs_ref[:, lanes] = silu(gp)

    def chunk(rr, lo=0, n=PLANES):
        return kv.at[pl.ds(lo, n), rr, :, pl.ds(HD, 2 * HD)]

    def fwd(s):
        ref = chunk(2 * ((z + ZN - s + 1) % ZN) + core, 0, 4 if s < 4 else 2)
        return remote(ref, ref, fwd_send.at[s], fwd_recv.at[s], at(plane, 2 * ((z + 1) % ZN) + core))

    def bwd(s):
        ref = chunk(2 * ((z + s - 1) % ZN) + core, 0 if s < 4 else 2, 4 if s < 4 else 2)
        return remote(ref, ref, bwd_send.at[s], bwd_recv.at[s], at(plane, 2 * ((z + ZN - 1) % ZN) + core))

    def sibling(s):
        ref = chunk(2 * ((z + ZN - s) % ZN) + core)
        return remote(ref, ref, sib_send.at[s], sib_recv.at[s], at(plane, 2 * z + 1 - core))

    def ring_first():
        for copy in own_qkv[:2]:
            copy.wait()
        for o in range(1, PLANES):
            for copy in qkv_copies(o, (0, 1)):
                copy.wait_recv()
        fwd(1).start()
        bwd(1).start()
        sibling(0).start()

    def ring_next(s):
        fwd(s).wait_recv()
        bwd(s).wait_recv()
        if s < 4:
            fwd(s + 1).start()
            bwd(s + 1).start()
            sibling(s).start()
            sibling(ZN - s).start()
        else:
            sibling(4).start()

    ring_first()

    sub = iota((8, 128), 0)

    def prefix_parts(lanes):
        total = cum_ref[pl.ds((STEPS - 1) * 8, 8), lanes]
        two = total + pltpu.roll(total, 1, 0)
        four = two + pltpu.roll(two, 2, 0)
        return total, two, four

    @pl.loop(0, CH // 128)
    def _(cb):
        for s in range(1, 4):
            @pl.when(cb == 8 * s)
            def _():
                ring_next(s)

        lanes = pl.ds(pl.multiple_of(cb * 128, 128), 128)
        total, two, four = prefix_parts(lanes)
        spans = [
            (1, jnp.where(sub >= 1, total, HUGE)),
            (2, jnp.where(sub >= 2, two, HUGE)),
            (4, jnp.where(sub >= 4, four, HUGE)),
        ]
        ys = [jnp.zeros((8, 128), F32) for _ in range(STEPS)]
        for n in range(NS):
            rate = rates_ref[n, :, lanes]
            state = jnp.zeros((8, 128), F32)
            for i in range(STEPS):
                rows = pl.ds(i * 8, 8)
                exponent = s_ref[rows, lanes] * rate
                factor = jnp.exp2(exponent)
                square = jnp.tanh(exponent * (-LN2)) * (1.0 + factor * factor)
                weight = square * lax.rsqrt(square)
                drive = u_ref[rows, lanes] * bb_ref[rows, pl.ds(n * 128, 128)]
                state = factor * state + weight * drive
                ys[i] = ys[i] + cc_ref[rows, pl.ds(n * 128, 128)] * state
            for by, span in spans:
                state = state + jnp.exp2(rate * span) * pltpu.roll(state, by, 0)
            totals[pl.ds(n, 1), lanes] = state[7:8]
            ends_ref[n, :, lanes] = jnp.where(sub >= 1, pltpu.roll(state, 1, 0), 0.0)
        for i in range(STEPS):
            y_ref[pl.ds(i * 8, 8), lanes] = ys[i]
        summed = total
        for by in (1, 2, 4):
            summed = summed + jnp.where(sub >= by, pltpu.roll(summed, by, 0), 0.0)
        totals[pl.ds(NS, 8), lanes] = jnp.broadcast_to(summed[7:8], (8, 128))

    def own_lanes(rr):
        return pl.ds(pl.multiple_of(rr * OWN, OWN), OWN)

    def totals_copy(j):
        rr = (r + j) % RING
        return remote(totals.at[:, own_lanes(rr)], plane_in.at[r], tot_send.at[j], tot_recv.at[j], at(plane, rr))

    @pl.loop(1, RING)
    def _(j):
        totals_copy(j).start()

    plane_in[r] = totals[:, own_lanes(r)]
    ring_next(4)

    for copy in own_qkv[2:]:
        copy.wait()
    for o in range(1, PLANES):
        for copy in qkv_copies(o, (2,)):
            copy.wait_recv()
    for p in range(PLANES):
        for h in range(GROUP):
            q_aug[p, pl.ds(h * ROWS, ROWS), pl.ds(HD, HD)] = q_in[p, :, pl.ds(h * HD, HD)]
    for s in range(ZN):
        sibling(s).wait_recv()

    CK = RING * ROWS

    def out_copy(p):
        return remote(
            o_buf.at[p],
            attended_hbm.at[:, pl.ds(pl.multiple_of(plane * GROUP * HD, HD), GROUP * HD)],
            o_send.at[p],
            o_recv.at[plane],
            at(p, r),
        )

    def own_out_copy(p):
        return pltpu.make_async_copy(
            o_buf.at[p],
            attended_hbm.at[:, pl.ds(pl.multiple_of(plane * GROUP * HD, HD), GROUP * HD)],
            own_sem.at[3],
        )

    def attend(p):
        def part(c, carry, last):
            top, acc, total = carry
            keys = kv[c, :, :, pl.ds(0, 2 * HD)].reshape(CK, 2 * HD)
            values = kv[c, :, :, pl.ds(2 * HD, HD)].reshape(CK, HD)
            scores = lax.dot_general(keys, q_aug[p], LANE_CONTRACT, preferred_element_type=F32)
            if last:
                limit = iota((CK, GROUP * ROWS), 1) % ROWS + r * ROWS
                scores = jnp.where(iota((CK, GROUP * ROWS), 0) <= limit, scores, MASKED)
            new_top = jnp.maximum(top, jnp.max(scores, axis=0, keepdims=True) * SCALE)
            probs = jnp.exp2(scores * SCALE - new_top)
            shrink = jnp.exp2(top - new_top)
            total = total * shrink + jnp.sum(probs, axis=0, keepdims=True)
            acc = acc * shrink + lax.dot_general(
                values, probs.astype(BF16), ROW_CONTRACT, preferred_element_type=F32
            )
            return new_top, acc, total

        carry = (
            jnp.full((1, GROUP * ROWS), MASKED, F32),
            jnp.zeros((HD, GROUP * ROWS), F32),
            jnp.zeros((1, GROUP * ROWS), F32),
        )
        carry = lax.fori_loop(0, p, lambda c, held: part(c, held, False), carry)
        _, acc, total = part(p, carry, True)
        result = acc / total
        for h in range(GROUP):
            o_buf[p, :, pl.ds(h * HD, HD)] = result[:, h * ROWS : (h + 1) * ROWS].T.astype(BF16)

        @pl.when(plane != p)
        def _():
            out_copy(p).start()

        @pl.when(plane == p)
        def _():
            own_out_copy(p).start()

    attend(3)

    @pl.loop(1, RING)
    def _(j):
        totals_copy(j).wait_recv()

    own_rates = rates_t[:, own_lanes(r)]
    state = jnp.zeros((NS, OWN), F32)
    length = jnp.zeros((1, OWN), F32)
    for i in range(RING):
        own_prefix[i, pl.ds(0, NS), :] = state
        own_prefix[i, pl.ds(NS, 8), :] = jnp.broadcast_to(length, (8, OWN))
        step = plane_in[i, pl.ds(NS, 1), :]
        state = jnp.exp2(own_rates * step) * state + plane_in[i, pl.ds(0, NS), :]
        length = length + step
    plane_total[pl.ds(0, NS), :] = state
    plane_total[pl.ds(NS, 8), :] = jnp.broadcast_to(length, (8, OWN))

    def across_copy(o):
        p = (plane + o) % PLANES
        return remote(plane_total, across_in.at[plane], acr_send.at[o], acr_recv.at[o], at(p, r))

    for o in range(1, PLANES):
        across_copy(o).start()
    across_in[plane] = plane_total[...]

    attend(1)

    for o in range(1, PLANES):
        across_copy(o).wait_recv()
    state = jnp.zeros((NS, OWN), F32)
    for p in range(PLANES - 1):
        moved = jnp.exp2(own_rates * across_in[p, pl.ds(NS, 1), :]) * state + across_in[p, pl.ds(0, NS), :]
        state = jnp.where(p < plane, moved, state)
    for i in range(RING):
        spread[i] = own_prefix[i, pl.ds(0, NS), :] + jnp.exp2(own_rates * own_prefix[i, pl.ds(NS, 1), :]) * state

    def spread_copy(j):
        rr = (r + j) % RING
        return remote(spread.at[rr], entering.at[:, own_lanes(r)], spr_send.at[j], spr_recv.at[j], at(plane, rr))

    @pl.loop(1, RING)
    def _(j):
        spread_copy(j).start()

    entering[:, own_lanes(r)] = spread[r]

    attend(2)
    attend(0)

    @pl.loop(1, RING)
    def _(j):
        spread_copy(j).wait_recv()

    @pl.loop(0, CH // 128)
    def _(cb):
        lanes = pl.ds(pl.multiple_of(cb * 128, 128), 128)
        total, _, _ = prefix_parts(lanes)
        summed = total
        for by in (1, 2, 4):
            summed = summed + jnp.where(sub >= by, pltpu.roll(summed, by, 0), 0.0)
        lead = jnp.where(sub >= 1, pltpu.roll(summed, 1, 0), 0.0)
        ys = [y_ref[pl.ds(i * 8, 8), lanes] for i in range(STEPS)]
        for n in range(NS):
            rate = rates_ref[n, :, lanes]
            state = jnp.exp2(rate * lead) * entering[pl.ds(n, 1), lanes] + ends_ref[n, :, lanes]
            for i in range(STEPS):
                rows = pl.ds(i * 8, 8)
                left = jnp.exp2(cum_ref[rows, lanes] * rate) * state
                ys[i] = ys[i] + cc_ref[rows, pl.ds(n * 128, 128)] * left
        skip = skip_ref[:, lanes]
        for i in range(STEPS):
            rows = pl.ds(i * 8, 8)
            y_ref[rows, lanes] = (ys[i] + skip * u_ref[rows, lanes]) * gs_ref[rows, lanes]

    @pl.loop(0, CH // 512)
    def _(b):
        lanes = pl.ds(pl.multiple_of(b * 512, 512), 512)
        back = lax.dot_general(perm_b, y_ref[:, lanes].astype(BF16), ROW_CONTRACT, preferred_element_type=F32)
        m_out[:, lanes] = back.astype(BF16)

    store = pltpu.make_async_copy(m_out, mixed_hbm, store_sem)
    store.start()

    for o in range(1, PLANES):
        for copy in qkv_copies(o):
            copy.wait_send()
        across_copy(o).wait_send()
    for s in range(1, 5):
        fwd(s).wait_send()
        bwd(s).wait_send()
    for s in range(ZN):
        sibling(s).wait_send()

    @pl.loop(1, RING)
    def _(j):
        totals_copy(j).wait_send()
        spread_copy(j).wait_send()

    for p in range(PLANES):
        @pl.when(plane != p)
        def _():
            out_copy(p).wait_send()
            pltpu.make_async_remote_copy(
                src_ref=o_buf.at[p],
                dst_ref=attended_hbm.at[:, pl.ds(p * GROUP * HD, GROUP * HD)],
                send_sem=o_send.at[p],
                recv_sem=o_recv.at[p],
                device_id=at(p, r),
                device_id_type=MESH,
            ).wait_recv()

        @pl.when(plane == p)
        def _():
            own_out_copy(p).wait()

    store.wait()


def on_device(
    mamba_input, gate_branch, step_size, decay_rates, input_map, output_map, mixing_weight, mixing_bias,
    skip_gain, segments, query_rows, key_rows, value_rows,
):
    hbm = pl.BlockSpec(memory_space=pl.ANY)
    vmem = pl.BlockSpec(memory_space=pltpu.VMEM)
    big = pltpu.VMEM((ROWS, CH), F32)
    dma = pltpu.SemaphoreType.DMA
    return pl.pallas_call(
        kernel,
        out_shape=(
            jax.ShapeDtypeStruct((ROWS, CH), BF16),
            jax.ShapeDtypeStruct((ROWS, PLANES * GROUP * HD), BF16),
        ),
        in_specs=[hbm] * 3 + [vmem] * 7 + [hbm] * 3,
        out_specs=(hbm, hbm),
        scratch_shapes=[
            pltpu.VMEM((ROWS, CH), BF16),
            pltpu.VMEM((ROWS, CH), BF16),
            pltpu.VMEM((ROWS, CH), BF16),
            pltpu.VMEM((16, CH), BF16),
            big, big, big, big, big,
            pltpu.VMEM((NS, 8, CH), F32),
            pltpu.VMEM((NS, 8, CH), F32),
            pltpu.VMEM((NS, CH), F32),
            pltpu.VMEM((ROWS, NS * 128), F32),
            pltpu.VMEM((ROWS, NS * 128), F32),
            pltpu.VMEM((4, ROWS, ROWS), F32),
            pltpu.VMEM((PLANES, RING, ROWS, 3 * HD), BF16),
            pltpu.VMEM((PLANES, ROWS, GROUP * HD), BF16),
            pltpu.VMEM((PLANES, GROUP * ROWS, 2 * HD), BF16),
            pltpu.VMEM((PLANES, ROWS, GROUP * HD), BF16),
            pltpu.VMEM((ROWS, CH), BF16),
            pltpu.VMEM((NS + 8, CH), F32),
            pltpu.VMEM((RING, NS + 8, OWN), F32),
            pltpu.VMEM((NS + 8, OWN), F32),
            pltpu.VMEM((PLANES, NS + 8, OWN), F32),
            pltpu.VMEM((RING, NS, OWN), F32),
            pltpu.VMEM((NS, CH), F32),
            pltpu.VMEM((RING, NS + 8, OWN), F32),
            dma((3,)), dma((2,)), dma((4, 3)), dma((4, 3)),
            dma((5,)), dma((5,)), dma((5,)), dma((5,)), dma((ZN,)), dma((ZN,)),
            dma((RING,)), dma((RING,)), dma((PLANES,)), dma((PLANES,)), dma((RING,)), dma((RING,)),
            dma((PLANES,)), dma((PLANES,)), dma((4,)), dma(()),
        ],
        compiler_params=pltpu.CompilerParams(
            collective_id=0, has_side_effects=True, vmem_limit_bytes=60 * 2**20
        ),
        name="mixer",
    )(
        mamba_input, gate_branch, step_size, decay_rates, input_map, output_map, mixing_weight,
        mixing_bias.reshape(1, CH), skip_gain.reshape(1, CH), segments.reshape(PLANES * RING, ROWS),
        query_rows, key_rows, value_rows,
    )


def solution(mesh):
    split = P(("dp", "ctx"), None)
    in_specs = (
        split, split, split, P("dp", None), split, split, P(), P(), P(), P("dp"), split, split, split,
    )
    return jax.shard_map(
        on_device, mesh=mesh, in_specs=in_specs, out_specs=(split, split), check_vma=False
    )
```

```python
import functools

import jax
import jax.numpy as jnp
from jax import lax
from jax.experimental import pallas as pl
from jax.experimental.pallas import tpu as pltpu
from jax.sharding import PartitionSpec as P

F32 = jnp.float32
BF16 = jnp.bfloat16
MESH = pl.DeviceIdType.MESH
LOG2E = 1.4426950408889634
LN2 = 0.6931471805599453

ROWS = 128
CH = 4096
NS = 16
PLANES = 4
RING = 16
ZN = 8
HD = 128
GROUP = 4
STEPS = 16
HUGE = 3e38
MASKED = -1e30
RING_EVERY = 2
RING_START = 2
STORES = 4
OWN = CH // RING
SCALE = LOG2E / HD**0.5
ROW_CONTRACT = (((0,), (0,)), ((), ()))
LANE_CONTRACT = (((1,), (1,)), ((), ()))


def iota(shape, dim):
    return lax.broadcasted_iota(jnp.int32, shape, dim)


def tree_sum(terms):
    while len(terms) > 1:
        terms = [a + b for a, b in zip(terms[::2], terms[1::2])]
    return terms[0]


def silu(v):
    return (0.5 * v) * (1.0 + jnp.tanh(0.5 * v))


def kernel(
    x_hbm, gate_hbm, step_hbm, decay_ref, in_ref, out_map_ref, taps_ref, bias_ref, skip_ref, seg_ref,
    q_hbm, k_hbm, v_hbm,
    mixed_hbm, attended_hbm,
    xv, gv, sv, halo, u_ref, s_ref, cum_ref, gs_ref, y_ref, ends_ref, rates_ref, rates_t, bb_ref, cc_ref,
    masks_ref, bias_row, kv, docs, q_in, q_aug, o_buf, m_out, lengths, plane_len, totals, plane_in, plane_total, across_in, spread, entering,
    own_prefix,
    load_sem, halo_sem, qkv_send, qkv_recv, fwd_send, fwd_recv, bwd_send, bwd_recv, sib_send, sib_recv,
    len_send, len_recv, tot_send, tot_recv, acr_send, acr_recv, spr_send, spr_recv, o_send, o_recv, own_sem, store_sem,
):
    dp = lax.axis_index("dp")
    me = lax.axis_index("ctx")
    plane = me // RING
    r = me % RING
    z = r // 2
    core = r % 2

    def at(p, rr):
        return (dp, p * RING + rr)

    def remote(src, dst, send, recv, target):
        return pltpu.make_async_remote_copy(
            src_ref=src, dst_ref=dst, send_sem=send, recv_sem=recv, device_id=target, device_id_type=MESH
        )

    loads = [
        pltpu.make_async_copy(x_hbm, xv, load_sem.at[0]),
        pltpu.make_async_copy(step_hbm, sv, load_sem.at[1]),
        pltpu.make_async_copy(gate_hbm, gv, load_sem.at[2]),
    ]
    for load in loads:
        load.start()

    barrier = pltpu.get_barrier_semaphore()

    @pl.loop(1, RING)
    def _(j):
        pl.semaphore_signal(barrier, inc=1, device_id=at(plane, (r + j) % RING), device_id_type=MESH)

    @pl.loop(1, PLANES)
    def _(j):
        pl.semaphore_signal(barrier, inc=1, device_id=at((plane + j) % PLANES, r), device_id_type=MESH)

    count = PLANES * RING
    pl.semaphore_signal(barrier, inc=1, device_id=(dp, (me + 1) % count), device_id_type=MESH)
    pl.semaphore_signal(barrier, inc=1, device_id=(dp, (me + count - 1) % count), device_id_type=MESH)
    unit = (iota((16, HD), 0) == iota((16, HD), 1)).astype(BF16)
    doc_ids = iota((16, ROWS), 0).astype(F32)

    @pl.loop(0, PLANES * RING // 8, unroll=True)
    def _(g):
        rows = seg_ref[pl.ds(pl.multiple_of(g * 8, 8), 8), :].astype(F32)
        for i in range(8):
            hot = (doc_ids == rows[i : i + 1]).astype(BF16)
            cols = lax.dot_general(hot, unit, ROW_CONTRACT, preferred_element_type=F32)
            docs[g // 2, (g % 2) * 8 + i] = cols.astype(BF16)

    pl.semaphore_wait(barrier, RING - 1 + PLANES - 1 + 2)

    halo_copy = remote(
        x_hbm.at[pl.ds(ROWS - 16, 16), :], halo, halo_sem.at[0], halo_sem.at[1], (dp, (me + 1) % count)
    )
    halo_copy.start()

    def qkv_parts(p):
        return [
            (k_hbm.at[:, pl.ds(pl.multiple_of(p * HD, HD), HD)], kv.at[r, plane, :, pl.ds(0, HD)]),
            (v_hbm.at[:, pl.ds(pl.multiple_of(p * HD, HD), HD)], kv.at[r, plane, :, pl.ds(HD, HD)]),
            (q_hbm.at[:, pl.ds(pl.multiple_of(p * GROUP * HD, HD), GROUP * HD)], q_in.at[plane]),
        ]

    def qkv_copies(o, parts=(0, 1, 2)):
        p = (plane + o) % PLANES
        pairs = qkv_parts(p)
        return [
            remote(pairs[i][0], pairs[i][1], qkv_send.at[o, i], qkv_recv.at[o, i], at(p, r)) for i in parts
        ]

    for o in range(1, PLANES):
        for copy in qkv_copies(o, (0, 1)):
            copy.start()
    own_qkv = [pltpu.make_async_copy(s, d, own_sem.at[i]) for i, (s, d) in enumerate(qkv_parts(plane))]
    for copy in own_qkv:
        copy.start()

    p_ids, t_ids = iota((ROWS, ROWS), 0), iota((ROWS, ROWS), 1)
    perm = (t_ids == (p_ids % 8) * STEPS + p_ids // 8).astype(F32)
    perm_b = perm.astype(BF16)
    ones = jnp.ones((ROWS, ROWS), BF16)

    seg = seg_ref[...].astype(F32)
    block_ids = iota((PLANES * RING, ROWS), 0)

    def seg_row(b):
        return jnp.sum(jnp.where(block_ids == b, seg, 0.0), axis=0, keepdims=True)

    here = jnp.broadcast_to(seg_row(me), (8, ROWS))
    before = jnp.broadcast_to(jnp.where(me > 0, seg_row(me - 1), -1.0), (8, ROWS))
    lane8 = iota((8, ROWS), 1)
    for d in range(1, 4):
        ids = jnp.where(lane8 >= d, pltpu.roll(here, d, 1), pltpu.roll(before, d, 1))
        same = (ids == here).astype(F32)
        masks_ref[d] = jnp.dot((perm * same[0:1]).astype(BF16), ones, preferred_element_type=F32)
        if d == 1:
            fresh = ((ids != here) & (ids >= 0.0)).astype(F32)
            masks_ref[0] = jnp.dot((perm * fresh[0:1]).astype(BF16), ones, preferred_element_type=F32)

    repeat = (iota((NS, NS * 128), 0) == iota((NS, NS * 128), 1) // 128).astype(BF16)
    for src, dst in ((in_ref, bb_ref), (out_map_ref, cc_ref)):
        ordered = lax.dot_general(src[...], perm_b, LANE_CONTRACT, preferred_element_type=F32).astype(BF16)
        dst[...] = lax.dot_general(ordered, repeat, ROW_CONTRACT, preferred_element_type=F32)

    bias = bias_ref[...].astype(F32)
    for i in range(CH // 128):
        bias_row[:, pl.ds(i * 128, 128)] = bias[i : i + 1]

    @pl.loop(0, CH // 128)
    def _(cb):
        lanes = pl.ds(pl.multiple_of(cb * 128, 128), 128)
        rates = jnp.minimum(decay_ref[:, lanes], -1e-30) * LOG2E
        rates_t[:, lanes] = rates
        for n in range(NS):
            rates_ref[n, :, lanes] = jnp.broadcast_to(rates[n : n + 1], (8, 128))

    for p in range(PLANES):
        ids = seg_row(p * RING + r)
        cold = jnp.where((doc_ids != ids) & (doc_ids < 4.0), MASKED, 0.0).astype(BF16)
        cols = lax.dot_general(cold, unit, ROW_CONTRACT, preferred_element_type=F32).astype(BF16)
        for h in range(GROUP):
            q_aug[p, pl.ds(h * ROWS, ROWS), pl.ds(0, HD)] = cols

    def own_lanes(rr):
        return pl.ds(pl.multiple_of(rr * OWN, OWN), OWN)

    def lengths_copy(j):
        rr = (r + j) % RING
        return remote(lengths.at[:, own_lanes(rr)], plane_len.at[r], len_send.at[j], len_recv.at[j], at(plane, rr))

    def piece(rr, c):
        return kv.at[rr, c]

    def fwd(s, c):
        ref = piece(2 * ((z + ZN - s + 1) % ZN) + core, c)
        return remote(ref, ref, fwd_send.at[s, c], fwd_recv.at[s, c], at(plane, 2 * ((z + 1) % ZN) + core))

    def bwd(s, c):
        ref = piece(2 * ((z + s - 1) % ZN) + core, c)
        return remote(ref, ref, bwd_send.at[s, c], bwd_recv.at[s, c], at(plane, 2 * ((z + ZN - 1) % ZN) + core))

    def sibling(s, c):
        ref = piece(2 * ((z + ZN - s) % ZN) + core, c)
        return remote(ref, ref, sib_send.at[s, c], sib_recv.at[s, c], at(plane, 2 * z + 1 - core))

    def ring(s, c):
        return ([fwd(s, c)] if s < 4 or c < 2 else []) + ([bwd(s, c)] if s < 4 or c >= 2 else [])

    def ring_first():
        for copy in own_qkv[:2]:
            copy.wait()
        for o in range(1, PLANES):
            for copy in qkv_copies(o, (0, 1)):
                copy.wait_recv()
        for c in range(PLANES):
            for copy in ring(1, c):
                copy.start()
        for c in range(PLANES):
            sibling(0, c).start()

    def ring_next(s, c):
        for copy in ring(s, c):
            copy.wait_recv()
        sibling(s, c).start()

    def ring_turn(k):
        s, c = 1 + k // PLANES, k % PLANES
        fwd(s, c).wait_recv()
        bwd(s, c).wait_recv()

        @pl.when((s < 3) | (c < 2))
        def _():
            fwd(s + 1, c).start()

        @pl.when((s < 3) | (c >= 2))
        def _():
            bwd(s + 1, c).start()

        sibling(s, c).start()
        sibling(ZN - s, c).start()

    def shared(c):
        for s in range(ZN):
            sibling(s, c).wait_recv()

    for load in loads:
        load.wait()
    W = 1024

    @pl.loop(0, CH // W)
    def _(b):
        lanes = pl.ds(pl.multiple_of(b * W, W), W)
        sp = jnp.dot(perm_b, sv[:, lanes], preferred_element_type=F32)
        gp = jnp.dot(perm_b, gv[:, lanes], preferred_element_type=F32)
        fresh = jnp.concatenate([masks_ref[0]] * (W // 128), axis=1)
        steps = jnp.where(fresh > 0.0, HUGE, sp)
        s_ref[:, lanes] = steps
        running = steps[0:8]
        cum_ref[pl.ds(0, 8), lanes] = running
        for i in range(1, STEPS):
            running = running + steps[i * 8 : i * 8 + 8]
            cum_ref[pl.ds(i * 8, 8), lanes] = running
        gs_ref[:, lanes] = silu(gp)
        for by in (1, 2, 4):
            running = running + jnp.where(iota((8, W), 0) >= by, pltpu.roll(running, by, 0), 0.0)
        lengths[:, lanes] = running[7:8]

    halo_copy.wait()

    @pl.loop(0, CH // W)
    def _(b):
        lanes = pl.ds(pl.multiple_of(b * W, W), W)
        xp = jnp.dot(perm_b, xv[:, lanes], preferred_element_type=F32)
        edge = halo[:, lanes].astype(F32)
        first = iota((8, W), 0) == 0
        lead = []
        for d in (3, 2, 1):
            rolled = pltpu.roll(xp[(STEPS - d) * 8 : (STEPS - d + 1) * 8], 1, 0)
            lead.append(jnp.where(first, edge[16 - d : 17 - d], rolled))
        extended = jnp.concatenate(lead + [xp], axis=0)
        taps = taps_ref[:, lanes].astype(F32)
        summed = bias_row[:, lanes] + taps[3:4] * xp
        for d in range(1, 4):
            allowed = jnp.concatenate([masks_ref[d]] * (W // 128), axis=1)
            earlier = extended[(3 - d) * 8 : (3 - d) * 8 + ROWS]
            summed = summed + taps[3 - d : 4 - d] * earlier * allowed
        u_ref[:, lanes] = silu(summed).astype(BF16).astype(F32)

    ring_first()
    for o in range(1, PLANES):
        for copy in qkv_copies(o, (2,)):
            copy.start()

    @pl.loop(1, RING)
    def _(j):
        lengths_copy(j).start()

    plane_len[r] = lengths[:, own_lanes(r)]

    sub = iota((8, 128), 0)

    def prefix_parts(lanes):
        total = cum_ref[pl.ds((STEPS - 1) * 8, 8), lanes]
        two = total + pltpu.roll(total, 1, 0)
        four = two + pltpu.roll(two, 2, 0)
        return total, two, four

    def scan(cb):
        lanes = pl.ds(pl.multiple_of(cb * 128, 128), 128)
        total, two, four = prefix_parts(lanes)
        spans = [
            (1, jnp.where(sub >= 1, total, HUGE)),
            (2, jnp.where(sub >= 2, two, HUGE)),
            (4, jnp.where(sub >= 4, four, HUGE)),
        ]
        rates = [rates_ref[n, :, lanes] for n in range(NS)]
        states = [jnp.zeros((8, 128), F32) for _ in range(NS)]
        for i in range(STEPS):
            rows = pl.ds(i * 8, 8)
            steps, drive = s_ref[rows, lanes], u_ref[rows, lanes]
            reads = []
            for n in range(NS):
                coef = pl.ds(n * 128, 128)
                exponent = steps * rates[n]
                factor = jnp.exp2(exponent)
                square = jnp.tanh(exponent * (-LN2)) * (1.0 + factor * factor)
                weight = square * lax.rsqrt(square)
                states[n] = factor * states[n] + weight * (drive * bb_ref[rows, coef])
                reads.append(cc_ref[rows, coef] * states[n])
            y_ref[rows, lanes] = tree_sum(reads)
        for n in range(NS):
            state = states[n]
            for by, span in spans:
                state = state + jnp.exp2(rates[n] * span) * pltpu.roll(state, by, 0)
            totals[pl.ds(n, 1), lanes] = state[7:8]
            ends_ref[n, :, lanes] = jnp.where(sub >= 1, pltpu.roll(state, 1, 0), 0.0)

    @pl.loop(0, CH // 128 // RING_EVERY)
    def _(group):
        @pl.when((group >= RING_START) & (group < RING_START + 3 * PLANES))
        def _():
            ring_turn(group - RING_START)

        pl.loop(group * RING_EVERY, (group + 1) * RING_EVERY)(scan)

    ring_next(4, 0)
    ring_next(4, 1)

    def totals_copy(j):
        rr = (r + j) % RING
        return remote(totals.at[:, own_lanes(rr)], plane_in.at[r], tot_send.at[j], tot_recv.at[j], at(plane, rr))

    @pl.loop(1, RING)
    def _(j):
        totals_copy(j).start()

    plane_in[r] = totals[:, own_lanes(r)]

    for copy in own_qkv[2:]:
        copy.wait()
    for o in range(1, PLANES):
        for copy in qkv_copies(o, (2,)):
            copy.wait_recv()
    for p in range(PLANES):
        for h in range(GROUP):
            q_aug[p, pl.ds(h * ROWS, ROWS), pl.ds(HD, HD)] = q_in[p, :, pl.ds(h * HD, HD)]
    shared(0)
    shared(1)

    CK = RING * ROWS

    def out_copy(p):
        return remote(
            o_buf.at[p],
            attended_hbm.at[:, pl.ds(pl.multiple_of(plane * GROUP * HD, HD), GROUP * HD)],
            o_send.at[p],
            o_recv.at[plane],
            at(p, r),
        )

    def own_out_copy(p):
        return pltpu.make_async_copy(
            o_buf.at[p],
            attended_hbm.at[:, pl.ds(pl.multiple_of(plane * GROUP * HD, HD), GROUP * HD)],
            own_sem.at[3],
        )

    def step_scores(p, c):
        keys = kv[:, c, :, pl.ds(0, HD)].reshape(CK, HD)
        keys = jnp.concatenate([docs[c].reshape(CK, HD), keys], axis=1)
        scores = lax.dot_general(keys, q_aug[p], LANE_CONTRACT, preferred_element_type=F32)
        if c == p:
            limit = iota((CK, GROUP * ROWS), 1) % ROWS + r * ROWS
            scores = jnp.where(iota((CK, GROUP * ROWS), 0) <= limit, scores, MASKED)
        return scores

    held = {}

    def step_rest(p, c, scores):
        values = kv[:, c, :, pl.ds(HD, HD)].reshape(CK, HD)
        top = jnp.max(scores, axis=0, keepdims=True) * SCALE
        if c > 0:
            old_top, old_acc, old_total = held[p]
            top = jnp.maximum(old_top, top)
        probs = jnp.exp2(scores * SCALE - top)
        total = jnp.sum(probs, axis=0, keepdims=True)
        acc = lax.dot_general(values, probs.astype(BF16), ROW_CONTRACT, preferred_element_type=F32)
        if c > 0:
            shrink = jnp.exp2(old_top - top)
            acc, total = old_acc * shrink + acc, old_total * shrink + total
        held[p] = top, acc, total
        if c < p:
            return
        result = acc / total
        for h in range(GROUP):
            o_buf[p, :, pl.ds(h * HD, HD)] = result[:, h * ROWS : (h + 1) * ROWS].T.astype(BF16)

        @pl.when(plane != p)
        def _():
            out_copy(p).start()

        @pl.when(plane == p)
        def _():
            own_out_copy(p).start()

    order = [(0, 0), (1, 0), (1, 1), (2, 0), (2, 1), (3, 0), (3, 1), (2, 2), (3, 2), (3, 3)]
    ahead = [step_scores(*order[0])]

    def attend(first, end):
        for k in range(first, end):
            scores = ahead.pop()
            if k + 1 < len(order):
                ahead.append(step_scores(*order[k + 1]))
            step_rest(*order[k], scores)

    attend(0, 3)
    ring_next(4, 2)
    ring_next(4, 3)
    attend(3, 4)

    @pl.loop(1, RING)
    def _(j):
        totals_copy(j).wait_recv()
        lengths_copy(j).wait_recv()

    own_rates = rates_t[:, own_lanes(r)]
    state = jnp.zeros((NS, OWN), F32)
    length = jnp.zeros((1, OWN), F32)
    for i in range(RING):
        own_prefix[i, pl.ds(0, NS), :] = state
        own_prefix[i, pl.ds(NS, 8), :] = jnp.broadcast_to(length, (8, OWN))
        step = plane_len[i]
        state = jnp.exp2(own_rates * step) * state + plane_in[i]
        length = length + step
    plane_total[pl.ds(0, NS), :] = state
    plane_total[pl.ds(NS, 8), :] = jnp.broadcast_to(length, (8, OWN))

    def across_copy(o):
        p = (plane + o) % PLANES
        return remote(plane_total, across_in.at[plane], acr_send.at[o], acr_recv.at[o], at(p, r))

    for o in range(1, PLANES):
        across_copy(o).start()
    across_in[plane] = plane_total[...]

    attend(4, 6)

    for o in range(1, PLANES):
        across_copy(o).wait_recv()
    state = jnp.zeros((NS, OWN), F32)
    for p in range(PLANES - 1):
        moved = jnp.exp2(own_rates * across_in[p, pl.ds(NS, 1), :]) * state + across_in[p, pl.ds(0, NS), :]
        state = jnp.where(p < plane, moved, state)
    for i in range(RING):
        moved = own_prefix[i, pl.ds(0, NS), :] + jnp.exp2(own_rates * own_prefix[i, pl.ds(NS, 1), :]) * state
        spread[i] = moved.astype(BF16)

    def spread_copy(j):
        rr = (r + j) % RING
        return remote(spread.at[rr], entering.at[:, own_lanes(r)], spr_send.at[j], spr_recv.at[j], at(plane, rr))

    @pl.loop(1, RING)
    def _(j):
        spread_copy(j).start()

    entering[:, own_lanes(r)] = spread[r]

    shared(2)
    shared(3)
    attend(6, 10)

    @pl.loop(1, RING)
    def _(j):
        spread_copy(j).wait_recv()

    def store(s):
        lanes = pl.ds(s * (CH // STORES), CH // STORES)
        return pltpu.make_async_copy(m_out.at[:, lanes], mixed_hbm.at[:, lanes], store_sem.at[s])

    def finish(cb):
        lanes = pl.ds(pl.multiple_of(cb * 128, 128), 128)
        total, _, _ = prefix_parts(lanes)
        summed = total
        for by in (1, 2, 4):
            summed = summed + jnp.where(sub >= by, pltpu.roll(summed, by, 0), 0.0)
        lead = jnp.where(sub >= 1, pltpu.roll(summed, 1, 0), 0.0)
        rates = [rates_ref[n, :, lanes] for n in range(NS)]
        arriving = entering[:, lanes].astype(F32)
        states = [jnp.exp2(rates[n] * lead) * arriving[n : n + 1] + ends_ref[n, :, lanes] for n in range(NS)]
        skip = skip_ref[:, lanes]
        for i in range(STEPS):
            rows = pl.ds(i * 8, 8)
            since = cum_ref[rows, lanes]
            reads = [
                cc_ref[rows, pl.ds(n * 128, 128)] * (jnp.exp2(since * rates[n]) * states[n]) for n in range(NS)
            ]
            readout = y_ref[rows, lanes] + tree_sum(reads)
            s_ref[rows, lanes] = (readout + skip * u_ref[rows, lanes]) * gs_ref[rows, lanes]

    back = (p_ids == (t_ids % 8) * STEPS + t_ids // 8).astype(BF16)
    for s in range(STORES):
        pl.loop(s * (CH // 128 // STORES), (s + 1) * (CH // 128 // STORES))(finish)
        lanes = pl.ds(s * (CH // STORES), CH // STORES)
        m_out[:, lanes] = jnp.dot(back, s_ref[:, lanes].astype(BF16), preferred_element_type=F32).astype(BF16)
        store(s).start()

    for o in range(1, PLANES):
        for copy in qkv_copies(o):
            copy.wait_send()
        across_copy(o).wait_send()
    for c in range(PLANES):
        for s in range(1, 5):
            for copy in ring(s, c):
                copy.wait_send()
        for s in range(ZN):
            sibling(s, c).wait_send()

    @pl.loop(1, RING)
    def _(j):
        totals_copy(j).wait_send()
        lengths_copy(j).wait_send()
        spread_copy(j).wait_send()

    for p in range(PLANES):
        @pl.when(plane != p)
        def _():
            out_copy(p).wait_send()
            pltpu.make_async_remote_copy(
                src_ref=o_buf.at[p],
                dst_ref=attended_hbm.at[:, pl.ds(p * GROUP * HD, GROUP * HD)],
                send_sem=o_send.at[p],
                recv_sem=o_recv.at[p],
                device_id=at(p, r),
                device_id_type=MESH,
            ).wait_recv()

        @pl.when(plane == p)
        def _():
            own_out_copy(p).wait()

    for s in range(STORES):
        store(s).wait()


def hand_over(mixed, attended, mixed_out, attended_out, mixed_buf, attended_buf, sem):
    inward, outward = [], []
    for src, buf, dst, pieces in ((mixed, mixed_buf, mixed_out, 4), (attended, attended_buf, attended_out, 2)):
        for i in range(pieces):
            lanes = pl.ds(i * 1024, 1024)
            inward.append(pltpu.make_async_copy(src.at[:, lanes], buf.at[:, lanes], sem.at[0, len(inward)]))
            outward.append(pltpu.make_async_copy(buf.at[:, lanes], dst.at[:, lanes], sem.at[1, len(outward)]))
    for copy in inward:
        copy.start()
    for arrival, copy in zip(inward, outward):
        arrival.wait()
        copy.start()
    for copy in outward:
        copy.wait()


def on_device(
    mamba_input, gate_branch, step_size, decay_rates, input_map, output_map, mixing_weight, mixing_bias,
    skip_gain, segments, query_rows, key_rows, value_rows,
):
    hbm = pl.BlockSpec(memory_space=pl.ANY)
    vmem = pl.BlockSpec(memory_space=pltpu.VMEM)
    big = pltpu.VMEM((ROWS, CH), F32)
    dma = pltpu.SemaphoreType.DMA
    mixed, attended = pl.pallas_call(
        kernel,
        out_shape=(
            jax.ShapeDtypeStruct((ROWS, CH), BF16),
            jax.ShapeDtypeStruct((ROWS, PLANES * GROUP * HD), BF16),
        ),
        in_specs=[hbm] * 3 + [vmem] * 7 + [hbm] * 3,
        out_specs=(hbm, hbm),
        scratch_shapes=[
            pltpu.VMEM((ROWS, CH), BF16),
            pltpu.VMEM((ROWS, CH), BF16),
            pltpu.VMEM((ROWS, CH), BF16),
            pltpu.VMEM((16, CH), BF16),
            big, big, big, big, big,
            pltpu.VMEM((NS, 8, CH), F32),
            pltpu.VMEM((NS, 8, CH), F32),
            pltpu.VMEM((NS, CH), F32),
            pltpu.VMEM((ROWS, NS * 128), F32),
            pltpu.VMEM((ROWS, NS * 128), F32),
            pltpu.VMEM((4, ROWS, ROWS), F32),
            pltpu.VMEM((1, CH), F32),
            pltpu.VMEM((RING, PLANES, ROWS, 2 * HD), BF16),
            pltpu.VMEM((PLANES, RING, ROWS, HD), BF16),
            pltpu.VMEM((PLANES, ROWS, GROUP * HD), BF16),
            pltpu.VMEM((PLANES, GROUP * ROWS, 2 * HD), BF16),
            pltpu.VMEM((PLANES, ROWS, GROUP * HD), BF16),
            pltpu.VMEM((ROWS, CH), BF16),
            pltpu.VMEM((1, CH), F32),
            pltpu.VMEM((RING, 1, OWN), F32),
            pltpu.VMEM((NS, CH), F32),
            pltpu.VMEM((RING, NS, OWN), F32),
            pltpu.VMEM((NS + 8, OWN), F32),
            pltpu.VMEM((PLANES, NS + 8, OWN), F32),
            pltpu.VMEM((RING, NS, OWN), BF16),
            pltpu.VMEM((NS, CH), BF16),
            pltpu.VMEM((RING, NS + 8, OWN), F32),
            dma((3,)), dma((2,)), dma((4, 3)), dma((4, 3)),
            dma((5, 4)), dma((5, 4)), dma((5, 4)), dma((5, 4)), dma((ZN, 4)), dma((ZN, 4)),
            dma((RING,)), dma((RING,)), dma((RING,)), dma((RING,)), dma((PLANES,)), dma((PLANES,)), dma((RING,)), dma((RING,)),
            dma((PLANES,)), dma((PLANES,)), dma((4,)), dma((STORES,)),
        ],
        compiler_params=pltpu.CompilerParams(
            collective_id=0, has_side_effects=True, vmem_limit_bytes=60 * 2**20
        ),
        name="mixer",
    )(
        mamba_input, gate_branch, step_size, decay_rates.T, input_map.T, output_map.T, mixing_weight,
        mixing_bias.reshape(CH // 128, 128), skip_gain.reshape(1, CH), segments.reshape(PLANES * RING, ROWS),
        query_rows, key_rows, value_rows,
    )
    shapes = (jax.ShapeDtypeStruct(mixed.shape, BF16), jax.ShapeDtypeStruct(attended.shape, BF16))
    return pl.pallas_call(
        hand_over,
        out_shape=shapes,
        in_specs=[hbm] * 2,
        out_specs=(hbm, hbm),
        scratch_shapes=[
            pltpu.VMEM(mixed.shape, BF16), pltpu.VMEM(attended.shape, BF16), dma((2, 6)),
        ],
        compiler_params=pltpu.CompilerParams(vmem_limit_bytes=60 * 2**20),
        name="hand_over",
    )(mixed, attended)


def solution(mesh):
    split = P(("dp", "ctx"), None)
    in_specs = (
        split, split, split, P("dp", None), split, split, P(), P(), P(), P("dp"), split, split, split,
    )
    return jax.shard_map(
        on_device, mesh=mesh, in_specs=in_specs, out_specs=(split, split), check_vma=False
    )
```

```python
import functools

import jax
import jax.numpy as jnp
from jax import lax
from jax.experimental import pallas as pl
from jax.experimental.pallas import tpu as pltpu
from jax.sharding import PartitionSpec as P

F32 = jnp.float32
BF16 = jnp.bfloat16
MESH = pl.DeviceIdType.MESH
LOG2E = 1.4426950408889634
LN2 = 0.6931471805599453

ROWS = 128
CH = 4096
NS = 16
PLANES = 4
RING = 16
ZN = 8
HD = 128
GROUP = 4
STEPS = 16
HUGE = 3e38
MASKED = -1e30
RING_EVERY = 1
RING_TURNS = (
    (3, 1, 0), (4, 1, 1), (6, 2, 0), (8, 2, 1), (9, 1, 2), (10, 3, 0), (11, 1, 3), (13, 2, 2), (14, 3, 1), (15, 2, 3)
)
RING_OWN = ((4, 2), (7, 3))
RING_END = 14
STORES = 4
OWN = CH // RING
SCALE = LOG2E / HD**0.5
ROW_CONTRACT = (((0,), (0,)), ((), ()))
LANE_CONTRACT = (((1,), (1,)), ((), ()))


def iota(shape, dim):
    return lax.broadcasted_iota(jnp.int32, shape, dim)


def tree_sum(terms):
    while len(terms) > 1:
        terms = [a + b for a, b in zip(terms[::2], terms[1::2])]
    return terms[0]


def silu(v):
    return (0.5 * v) * (1.0 + jnp.tanh(0.5 * v))


def kernel(
    x_hbm, gate_hbm, step_hbm, decay_ref, in_ref, out_map_ref, taps_ref, bias_ref, skip_ref, seg_ref,
    q_hbm, k_hbm, v_hbm,
    mixed_hbm, attended_hbm,
    xv, gv, sv, halo, u_ref, s_ref, cum_ref, gs_ref, y_ref, ends_ref, rates_ref, rates_t, bb_ref, cc_ref,
    masks_ref, bias_row, kv, docs, q_in, q_aug, o_buf, m_out, lengths, plane_len, totals, plane_in, plane_total, across_in, entered, spread, entering,
    own_prefix,
    load_sem, halo_sem, qkv_send, qkv_recv, fwd_send, fwd_recv, bwd_send, bwd_recv, sib_send, sib_recv,
    len_send, len_recv, tot_send, tot_recv, acr_send, acr_recv, spr_send, spr_recv, o_send, o_recv, own_sem, store_sem,
):
    dp = lax.axis_index("dp")
    me = lax.axis_index("ctx")
    plane = me // RING
    r = me % RING
    z = r // 2
    core = r % 2

    def at(p, rr):
        return (dp, p * RING + rr)

    def remote(src, dst, send, recv, target):
        return pltpu.make_async_remote_copy(
            src_ref=src, dst_ref=dst, send_sem=send, recv_sem=recv, device_id=target, device_id_type=MESH
        )

    loads = [
        pltpu.make_async_copy(x_hbm, xv, load_sem.at[0]),
        pltpu.make_async_copy(step_hbm, sv, load_sem.at[1]),
        pltpu.make_async_copy(gate_hbm, gv, load_sem.at[2]),
    ]
    for load in loads:
        load.start()

    barrier = pltpu.get_barrier_semaphore()

    @pl.loop(1, RING)
    def _(j):
        pl.semaphore_signal(barrier, inc=1, device_id=at(plane, (r + j) % RING), device_id_type=MESH)

    @pl.loop(1, PLANES)
    def _(j):
        pl.semaphore_signal(barrier, inc=1, device_id=at((plane + j) % PLANES, r), device_id_type=MESH)

    count = PLANES * RING
    pl.semaphore_signal(barrier, inc=1, device_id=(dp, (me + 1) % count), device_id_type=MESH)
    pl.semaphore_signal(barrier, inc=1, device_id=(dp, (me + count - 1) % count), device_id_type=MESH)
    unit = (iota((16, HD), 0) == iota((16, HD), 1)).astype(BF16)
    doc_ids = iota((16, ROWS), 0).astype(F32)

    @pl.loop(0, PLANES * RING // 8, unroll=True)
    def _(g):
        rows = seg_ref[pl.ds(pl.multiple_of(g * 8, 8), 8), :].astype(F32)
        for i in range(8):
            hot = (doc_ids == rows[i : i + 1]).astype(BF16)
            cols = lax.dot_general(hot, unit, ROW_CONTRACT, preferred_element_type=F32)
            docs[g // 2, (g % 2) * 8 + i] = cols.astype(BF16)

    pl.semaphore_wait(barrier, RING - 1 + PLANES - 1 + 2)

    halo_copy = remote(
        x_hbm.at[pl.ds(ROWS - 16, 16), :], halo, halo_sem.at[0], halo_sem.at[1], (dp, (me + 1) % count)
    )
    halo_copy.start()

    def qkv_parts(p):
        return [
            (k_hbm.at[:, pl.ds(pl.multiple_of(p * HD, HD), HD)], kv.at[r, plane, :, pl.ds(0, HD)]),
            (v_hbm.at[:, pl.ds(pl.multiple_of(p * HD, HD), HD)], kv.at[r, plane, :, pl.ds(HD, HD)]),
            (q_hbm.at[:, pl.ds(pl.multiple_of(p * GROUP * HD, HD), GROUP * HD)], q_in.at[plane]),
        ]

    def qkv_copies(o, parts=(0, 1, 2)):
        p = (plane + o) % PLANES
        pairs = qkv_parts(p)
        return [
            remote(pairs[i][0], pairs[i][1], qkv_send.at[o, i], qkv_recv.at[o, i], at(p, r)) for i in parts
        ]

    for o in range(1, PLANES):
        for copy in qkv_copies(o, (0, 1)):
            copy.start()
    own_qkv = [pltpu.make_async_copy(s, d, own_sem.at[i]) for i, (s, d) in enumerate(qkv_parts(plane))]
    for copy in own_qkv:
        copy.start()

    p_ids, t_ids = iota((ROWS, ROWS), 0), iota((ROWS, ROWS), 1)
    perm = (t_ids == (p_ids % 8) * STEPS + p_ids // 8).astype(F32)
    perm_b = perm.astype(BF16)
    ones = jnp.ones((ROWS, ROWS), BF16)

    seg = seg_ref[...].astype(F32)
    block_ids = iota((PLANES * RING, ROWS), 0)

    def seg_row(b):
        return jnp.sum(jnp.where(block_ids == b, seg, 0.0), axis=0, keepdims=True)

    here = jnp.broadcast_to(seg_row(me), (8, ROWS))
    before = jnp.broadcast_to(jnp.where(me > 0, seg_row(me - 1), -1.0), (8, ROWS))
    lane8 = iota((8, ROWS), 1)
    for d in range(1, 4):
        ids = jnp.where(lane8 >= d, pltpu.roll(here, d, 1), pltpu.roll(before, d, 1))
        same = (ids == here).astype(F32)
        masks_ref[d] = jnp.dot((perm * same[0:1]).astype(BF16), ones, preferred_element_type=F32)
        if d == 1:
            fresh = ((ids != here) & (ids >= 0.0)).astype(F32)
            masks_ref[0] = jnp.dot((perm * fresh[0:1]).astype(BF16), ones, preferred_element_type=F32)

    repeat = (iota((NS, NS * 128), 0) == iota((NS, NS * 128), 1) // 128).astype(BF16)
    for src, dst in ((in_ref, bb_ref), (out_map_ref, cc_ref)):
        ordered = lax.dot_general(src[...], perm_b, LANE_CONTRACT, preferred_element_type=F32).astype(BF16)
        dst[...] = lax.dot_general(ordered, repeat, ROW_CONTRACT, preferred_element_type=F32)

    bias = bias_ref[...].astype(F32)
    for i in range(CH // 128):
        bias_row[:, pl.ds(i * 128, 128)] = bias[i : i + 1]

    @pl.loop(0, CH // 128)
    def _(cb):
        lanes = pl.ds(pl.multiple_of(cb * 128, 128), 128)
        rates = jnp.minimum(decay_ref[:, lanes], -1e-30) * LOG2E
        rates_t[:, lanes] = rates
        for n in range(NS):
            rates_ref[n, :, lanes] = jnp.broadcast_to(rates[n : n + 1], (8, 128))

    for p in range(PLANES):
        ids = seg_row(p * RING + r)
        cold = jnp.where((doc_ids != ids) & (doc_ids < 4.0), MASKED, 0.0).astype(BF16)
        cols = lax.dot_general(cold, unit, ROW_CONTRACT, preferred_element_type=F32).astype(BF16)
        for h in range(GROUP):
            q_aug[p, pl.ds(h * ROWS, ROWS), pl.ds(0, HD)] = cols

    def own_lanes(rr):
        return pl.ds(pl.multiple_of(rr * OWN, OWN), OWN)

    def lengths_copy(j):
        rr = (r + j) % RING
        return remote(lengths.at[:, own_lanes(rr)], plane_len.at[r], len_send.at[j], len_recv.at[j], at(plane, rr))

    def piece(rr, c):
        return kv.at[rr, c]

    def fwd(s, c):
        ref = piece(2 * ((z + ZN - s + 1) % ZN) + core, c)
        return remote(ref, ref, fwd_send.at[s, c], fwd_recv.at[s, c], at(plane, 2 * ((z + 1) % ZN) + core))

    def bwd(s, c):
        ref = piece(2 * ((z + s - 1) % ZN) + core, c)
        return remote(ref, ref, bwd_send.at[s, c], bwd_recv.at[s, c], at(plane, 2 * ((z + ZN - 1) % ZN) + core))

    def sibling(s, c):
        ref = piece(2 * ((z + ZN - s) % ZN) + core, c)
        return remote(ref, ref, sib_send.at[s, c], sib_recv.at[s, c], at(plane, 2 * z + 1 - core))

    def ring(s, c):
        return ([fwd(s, c)] if s < 4 or c < 2 else []) + ([bwd(s, c)] if s < 4 or c >= 2 else [])

    def own_piece(c):
        for copy in ring(1, c):
            copy.start()

    def ring_first():
        for copy in own_qkv[:2]:
            copy.wait()
        for o in range(1, PLANES):
            for copy in qkv_copies(o, (0, 1)):
                copy.wait_recv()
        for c in (0, 1):
            own_piece(c)
        for c in range(PLANES):
            sibling(0, c).start()

    def ring_turn(s, c):
        fwd(s, c).wait_recv()
        bwd(s, c).wait_recv()

        @pl.when((s < 3) | (c < 2))
        def _():
            fwd(s + 1, c).start()

        @pl.when((s < 3) | (c >= 2))
        def _():
            bwd(s + 1, c).start()

        sibling(s, c).start()
        sibling(ZN - s, c).start()

    def ring_last(c):
        for copy in ring(4, c):
            copy.wait_recv()
        sibling(4, c).start()

    def shared(c):
        for s in range(ZN):
            sibling(s, c).wait_recv()

    for load in loads:
        load.wait()
    W = 1024

    @pl.loop(0, CH // W)
    def _(b):
        lanes = pl.ds(pl.multiple_of(b * W, W), W)
        sp = jnp.dot(perm_b, sv[:, lanes], preferred_element_type=F32)
        gp = jnp.dot(perm_b, gv[:, lanes], preferred_element_type=F32)
        fresh = jnp.concatenate([masks_ref[0]] * (W // 128), axis=1)
        steps = jnp.where(fresh > 0.0, HUGE, sp)
        s_ref[:, lanes] = steps
        running = steps[0:8]
        cum_ref[pl.ds(0, 8), lanes] = running
        for i in range(1, STEPS):
            running = running + steps[i * 8 : i * 8 + 8]
            cum_ref[pl.ds(i * 8, 8), lanes] = running
        gs_ref[:, lanes] = silu(gp)
        for by in (1, 2, 4):
            running = running + jnp.where(iota((8, W), 0) >= by, pltpu.roll(running, by, 0), 0.0)
        lengths[:, lanes] = running[7:8]

    halo_copy.wait()

    @pl.loop(0, CH // W)
    def _(b):
        lanes = pl.ds(pl.multiple_of(b * W, W), W)
        xp = jnp.dot(perm_b, xv[:, lanes], preferred_element_type=F32)
        edge = halo[:, lanes].astype(F32)
        first = iota((8, W), 0) == 0
        lead = []
        for d in (3, 2, 1):
            rolled = pltpu.roll(xp[(STEPS - d) * 8 : (STEPS - d + 1) * 8], 1, 0)
            lead.append(jnp.where(first, edge[16 - d : 17 - d], rolled))
        extended = jnp.concatenate(lead + [xp], axis=0)
        taps = taps_ref[:, lanes].astype(F32)
        summed = bias_row[:, lanes] + taps[3:4] * xp
        for d in range(1, 4):
            allowed = jnp.concatenate([masks_ref[d]] * (W // 128), axis=1)
            earlier = extended[(3 - d) * 8 : (3 - d) * 8 + ROWS]
            summed = summed + taps[3 - d : 4 - d] * earlier * allowed
        u_ref[:, lanes] = silu(summed).astype(BF16).astype(F32)

    ring_first()
    for o in range(1, PLANES):
        for copy in qkv_copies(o, (2,)):
            copy.start()

    @pl.loop(1, RING)
    def _(j):
        lengths_copy(j).start()

    plane_len[r] = lengths[:, own_lanes(r)]

    sub = iota((8, 128), 0)

    def prefix_parts(lanes):
        total = cum_ref[pl.ds((STEPS - 1) * 8, 8), lanes]
        two = total + pltpu.roll(total, 1, 0)
        four = two + pltpu.roll(two, 2, 0)
        return total, two, four

    def scan(pair):
        blocks = [pl.ds(pl.multiple_of(pair * 256 + b * 128, 128), 128) for b in range(2)]
        spans = []
        for lanes in blocks:
            total, two, four = prefix_parts(lanes)
            spans.append([
                (1, jnp.where(sub >= 1, total, HUGE)),
                (2, jnp.where(sub >= 2, two, HUGE)),
                (4, jnp.where(sub >= 4, four, HUGE)),
            ])
        for first in range(0, NS, NS // 2):
            held_states = range(first, first + NS // 2)
            rates = [[rates_ref[n, :, lanes] for n in held_states] for lanes in blocks]
            states = [[jnp.zeros((8, 128), F32) for n in held_states] for lanes in blocks]
            for i in range(STEPS):
                rows = pl.ds(i * 8, 8)
                steps = [s_ref[rows, lanes] for lanes in blocks]
                drives = [u_ref[rows, lanes] for lanes in blocks]
                reads = [[], []]
                for k, n in enumerate(held_states):
                    into = bb_ref[rows, pl.ds(n * 128, 128)]
                    out_of = cc_ref[rows, pl.ds(n * 128, 128)]
                    for b in range(2):
                        exponent = steps[b] * rates[b][k]
                        factor = jnp.exp2(exponent)
                        ratio = jnp.tanh(exponent * (-0.5 * LN2))
                        part = ratio * lax.rsqrt(ratio) * (drives[b] * into)
                        states[b][k] = factor * (states[b][k] + part) + part
                        reads[b].append(out_of * states[b][k])
                for b, lanes in enumerate(blocks):
                    readout = tree_sum(reads[b])
                    y_ref[rows, lanes] = readout if first == 0 else y_ref[rows, lanes] + readout
            for b, lanes in enumerate(blocks):
                for k, n in enumerate(held_states):
                    state = states[b][k]
                    for by, span in spans[b]:
                        state = state + jnp.exp2(rates[b][k] * span) * pltpu.roll(state, by, 0)
                    totals[pl.ds(n, 1), lanes] = state[7:8]
                    ends_ref[n, :, lanes] = jnp.where(sub >= 1, pltpu.roll(state, 1, 0), 0.0)

    @pl.loop(0, CH // 256 // RING_EVERY)
    def _(group):
        code = sum(jnp.where(group == look, s * PLANES + c, 0) for look, s, c in RING_TURNS)

        @pl.when(code > 0)
        def _():
            ring_turn(code // PLANES, code % PLANES)

        for look, c in RING_OWN:
            @pl.when(group == look)
            def _():
                own_piece(c)

        @pl.when(group == RING_END)
        def _():
            ring_last(0)

        pl.loop(group * RING_EVERY, (group + 1) * RING_EVERY)(scan)

    def totals_copy(j):
        rr = (r + j) % RING
        return remote(totals.at[:, own_lanes(rr)], plane_in.at[r], tot_send.at[j], tot_recv.at[j], at(plane, rr))

    @pl.loop(1, RING)
    def _(j):
        totals_copy(j).start()

    plane_in[r] = totals[:, own_lanes(r)]

    for copy in own_qkv[2:]:
        copy.wait()
    for o in range(1, PLANES):
        for copy in qkv_copies(o, (2,)):
            copy.wait_recv()
    for p in range(PLANES):
        for h in range(GROUP):
            q_aug[p, pl.ds(h * ROWS, ROWS), pl.ds(HD, HD)] = q_in[p, :, pl.ds(h * HD, HD)]
    shared(0)

    CK = RING * ROWS

    def out_copy(p):
        return remote(
            o_buf.at[p],
            attended_hbm.at[:, pl.ds(pl.multiple_of(plane * GROUP * HD, HD), GROUP * HD)],
            o_send.at[p],
            o_recv.at[plane],
            at(p, r),
        )

    def own_out_copy(p):
        return pltpu.make_async_copy(
            o_buf.at[p],
            attended_hbm.at[:, pl.ds(pl.multiple_of(plane * GROUP * HD, HD), GROUP * HD)],
            own_sem.at[3],
        )

    def step_scores(p, c):
        keys = kv[:, c, :, pl.ds(0, HD)].reshape(CK, HD)
        keys = jnp.concatenate([docs[c].reshape(CK, HD), keys], axis=1)
        scores = lax.dot_general(keys, q_aug[p], LANE_CONTRACT, preferred_element_type=F32)
        if c == p:
            limit = iota((CK, GROUP * ROWS), 1) % ROWS + r * ROWS
            scores = jnp.where(iota((CK, GROUP * ROWS), 0) <= limit, scores, MASKED)
        return scores

    held = {}

    def step_rest(p, c, scores):
        values = kv[:, c, :, pl.ds(HD, HD)].reshape(CK, HD)
        top = jnp.max(scores, axis=0, keepdims=True) * SCALE
        if c > 0:
            old_top, old_acc, old_total = held[p]
            top = jnp.maximum(old_top, top)
        probs = jnp.exp2(scores * SCALE - top)
        total = jnp.sum(probs, axis=0, keepdims=True)
        acc = lax.dot_general(values, probs.astype(BF16), ROW_CONTRACT, preferred_element_type=F32)
        if c > 0:
            shrink = jnp.exp2(old_top - top)
            acc, total = old_acc * shrink + acc, old_total * shrink + total
        held[p] = top, acc, total
        if c < p:
            return
        result = acc / total
        for h in range(GROUP):
            o_buf[p, :, pl.ds(h * HD, HD)] = result[:, h * ROWS : (h + 1) * ROWS].T.astype(BF16)

        @pl.when(plane != p)
        def _():
            out_copy(p).start()

        @pl.when(plane == p)
        def _():
            own_out_copy(p).start()

    order = [(0, 0), (1, 0), (2, 0), (3, 0), (1, 1), (2, 1), (3, 1), (2, 2), (3, 2), (3, 3)]
    ahead = [step_scores(*order[0])]

    def attend(first, end):
        for k in range(first, end):
            scores = ahead.pop()
            if k + 1 < len(order):
                ahead.append(step_scores(*order[k + 1]))
            step_rest(*order[k], scores)

    attend(0, 1)
    ring_turn(3, 2)
    attend(1, 2)
    ring_last(1)
    ring_turn(3, 3)
    attend(2, 3)

    @pl.loop(1, RING)
    def _(j):
        totals_copy(j).wait_recv()
        lengths_copy(j).wait_recv()

    own_rates = rates_t[:, own_lanes(r)]
    state = jnp.zeros((NS, OWN), F32)
    length = jnp.zeros((1, OWN), F32)
    for i in range(RING):
        own_prefix[i, pl.ds(0, NS), :] = state
        own_prefix[i, pl.ds(NS, 8), :] = jnp.broadcast_to(length, (8, OWN))
        step = plane_len[i]
        state = jnp.exp2(own_rates * step) * state + plane_in[i]
        length = length + step
    plane_total[pl.ds(0, NS), :] = state
    plane_total[pl.ds(NS, 8), :] = jnp.broadcast_to(length, (8, OWN))

    def across_copy(o):
        p = (plane + o) % PLANES
        return remote(plane_total, across_in.at[plane], acr_send.at[o], acr_recv.at[o], at(p, r))

    for o in range(1, PLANES):
        across_copy(o).start()

    shared(1)
    attend(3, 4)
    ring_last(2)
    attend(4, 5)
    ring_last(3)
    attend(5, 6)
    shared(2)

    for o in range(1, PLANES):
        @pl.when(o <= plane)
        def _():
            across_copy(o).wait_recv()

    entered[...] = jnp.zeros((NS, OWN), F32)
    for p in range(PLANES - 1):
        @pl.when(p < plane)
        def _():
            moved = jnp.exp2(own_rates * across_in[p, pl.ds(NS, 1), :]) * entered[...]
            entered[...] = moved + across_in[p, pl.ds(0, NS), :]

    state = entered[...]
    for i in range(RING):
        moved = own_prefix[i, pl.ds(0, NS), :] + jnp.exp2(own_rates * own_prefix[i, pl.ds(NS, 1), :]) * state
        spread[i] = moved.astype(BF16)

    def spread_copy(j):
        rr = (r + j) % RING
        return remote(spread.at[rr], entering.at[:, own_lanes(r)], spr_send.at[j], spr_recv.at[j], at(plane, rr))

    @pl.loop(1, RING)
    def _(j):
        spread_copy(j).start()

    entering[:, own_lanes(r)] = spread[r]

    attend(6, 8)
    shared(3)
    attend(8, 10)

    @pl.loop(1, RING)
    def _(j):
        spread_copy(j).wait_recv()

    def store(s):
        lanes = pl.ds(s * (CH // STORES), CH // STORES)
        return pltpu.make_async_copy(m_out.at[:, lanes], mixed_hbm.at[:, lanes], store_sem.at[s])

    def finish(cb):
        lanes = pl.ds(pl.multiple_of(cb * 128, 128), 128)
        total, _, _ = prefix_parts(lanes)
        summed = total
        for by in (1, 2, 4):
            summed = summed + jnp.where(sub >= by, pltpu.roll(summed, by, 0), 0.0)
        lead = jnp.where(sub >= 1, pltpu.roll(summed, 1, 0), 0.0)
        rates = [rates_ref[n, :, lanes] for n in range(NS)]
        arriving = entering[:, lanes].astype(F32)
        states = [jnp.exp2(rates[n] * lead) * arriving[n : n + 1] + ends_ref[n, :, lanes] for n in range(NS)]
        skip = skip_ref[:, lanes]
        for i in range(STEPS):
            rows = pl.ds(i * 8, 8)
            since = cum_ref[rows, lanes]
            reads = [
                cc_ref[rows, pl.ds(n * 128, 128)] * (jnp.exp2(since * rates[n]) * states[n]) for n in range(NS)
            ]
            readout = y_ref[rows, lanes] + tree_sum(reads)
            s_ref[rows, lanes] = (readout + skip * u_ref[rows, lanes]) * gs_ref[rows, lanes]

    back = (p_ids == (t_ids % 8) * STEPS + t_ids // 8).astype(BF16)
    for s in range(STORES):
        pl.loop(s * (CH // 128 // STORES), (s + 1) * (CH // 128 // STORES))(finish)
        lanes = pl.ds(s * (CH // STORES), CH // STORES)
        m_out[:, lanes] = jnp.dot(back, s_ref[:, lanes].astype(BF16), preferred_element_type=F32).astype(BF16)
        store(s).start()

    for o in range(1, PLANES):
        for copy in qkv_copies(o):
            copy.wait_send()
        across_copy(o).wait_send()

        @pl.when(o > plane)
        def _():
            across_copy(o).wait_recv()

    for c in range(PLANES):
        for s in range(1, 5):
            for copy in ring(s, c):
                copy.wait_send()
        for s in range(ZN):
            sibling(s, c).wait_send()

    @pl.loop(1, RING)
    def _(j):
        totals_copy(j).wait_send()
        lengths_copy(j).wait_send()
        spread_copy(j).wait_send()

    for p in range(PLANES):
        @pl.when(plane != p)
        def _():
            out_copy(p).wait_send()
            pltpu.make_async_remote_copy(
                src_ref=o_buf.at[p],
                dst_ref=attended_hbm.at[:, pl.ds(p * GROUP * HD, GROUP * HD)],
                send_sem=o_send.at[p],
                recv_sem=o_recv.at[p],
                device_id=at(p, r),
                device_id_type=MESH,
            ).wait_recv()

        @pl.when(plane == p)
        def _():
            own_out_copy(p).wait()

    for s in range(STORES):
        store(s).wait()


def hand_over(mixed, attended, mixed_out, attended_out, mixed_buf, attended_buf, sem):
    inward, outward = [], []
    for src, buf, dst, pieces in ((mixed, mixed_buf, mixed_out, 4), (attended, attended_buf, attended_out, 2)):
        for i in range(pieces):
            lanes = pl.ds(i * 1024, 1024)
            inward.append(pltpu.make_async_copy(src.at[:, lanes], buf.at[:, lanes], sem.at[0, len(inward)]))
            outward.append(pltpu.make_async_copy(buf.at[:, lanes], dst.at[:, lanes], sem.at[1, len(outward)]))
    for copy in inward:
        copy.start()
    for arrival, copy in zip(inward, outward):
        arrival.wait()
        copy.start()
    for copy in outward:
        copy.wait()


def on_device(
    mamba_input, gate_branch, step_size, decay_rates, input_map, output_map, mixing_weight, mixing_bias,
    skip_gain, segments, query_rows, key_rows, value_rows,
):
    hbm = pl.BlockSpec(memory_space=pl.ANY)
    vmem = pl.BlockSpec(memory_space=pltpu.VMEM)
    big = pltpu.VMEM((ROWS, CH), F32)
    dma = pltpu.SemaphoreType.DMA
    mixed, attended = pl.pallas_call(
        kernel,
        out_shape=(
            jax.ShapeDtypeStruct((ROWS, CH), BF16),
            jax.ShapeDtypeStruct((ROWS, PLANES * GROUP * HD), BF16),
        ),
        in_specs=[hbm] * 3 + [vmem] * 7 + [hbm] * 3,
        out_specs=(hbm, hbm),
        scratch_shapes=[
            pltpu.VMEM((ROWS, CH), BF16),
            pltpu.VMEM((ROWS, CH), BF16),
            pltpu.VMEM((ROWS, CH), BF16),
            pltpu.VMEM((16, CH), BF16),
            big, big, big, big, big,
            pltpu.VMEM((NS, 8, CH), F32),
            pltpu.VMEM((NS, 8, CH), F32),
            pltpu.VMEM((NS, CH), F32),
            pltpu.VMEM((ROWS, NS * 128), F32),
            pltpu.VMEM((ROWS, NS * 128), F32),
            pltpu.VMEM((4, ROWS, ROWS), F32),
            pltpu.VMEM((1, CH), F32),
            pltpu.VMEM((RING, PLANES, ROWS, 2 * HD), BF16),
            pltpu.VMEM((PLANES, RING, ROWS, HD), BF16),
            pltpu.VMEM((PLANES, ROWS, GROUP * HD), BF16),
            pltpu.VMEM((PLANES, GROUP * ROWS, 2 * HD), BF16),
            pltpu.VMEM((PLANES, ROWS, GROUP * HD), BF16),
            pltpu.VMEM((ROWS, CH), BF16),
            pltpu.VMEM((1, CH), F32),
            pltpu.VMEM((RING, 1, OWN), F32),
            pltpu.VMEM((NS, CH), F32),
            pltpu.VMEM((RING, NS, OWN), F32),
            pltpu.VMEM((NS + 8, OWN), F32),
            pltpu.VMEM((PLANES, NS + 8, OWN), F32),
            pltpu.VMEM((NS, OWN), F32),
            pltpu.VMEM((RING, NS, OWN), BF16),
            pltpu.VMEM((NS, CH), BF16),
            pltpu.VMEM((RING, NS + 8, OWN), F32),
            dma((3,)), dma((2,)), dma((4, 3)), dma((4, 3)),
            dma((5, 4)), dma((5, 4)), dma((5, 4)), dma((5, 4)), dma((ZN, 4)), dma((ZN, 4)),
            dma((RING,)), dma((RING,)), dma((RING,)), dma((RING,)), dma((PLANES,)), dma((PLANES,)), dma((RING,)), dma((RING,)),
            dma((PLANES,)), dma((PLANES,)), dma((4,)), dma((STORES,)),
        ],
        compiler_params=pltpu.CompilerParams(
            collective_id=0, has_side_effects=True, vmem_limit_bytes=60 * 2**20
        ),
        name="mixer",
    )(
        mamba_input, gate_branch, step_size, decay_rates.T, input_map.T, output_map.T, mixing_weight,
        mixing_bias.reshape(CH // 128, 128), skip_gain.reshape(1, CH), segments.reshape(PLANES * RING, ROWS),
        query_rows, key_rows, value_rows,
    )
    shapes = (jax.ShapeDtypeStruct(mixed.shape, BF16), jax.ShapeDtypeStruct(attended.shape, BF16))
    return pl.pallas_call(
        hand_over,
        out_shape=shapes,
        in_specs=[hbm] * 2,
        out_specs=(hbm, hbm),
        scratch_shapes=[
            pltpu.VMEM(mixed.shape, BF16), pltpu.VMEM(attended.shape, BF16), dma((2, 6)),
        ],
        compiler_params=pltpu.CompilerParams(vmem_limit_bytes=60 * 2**20),
        name="hand_over",
    )(mixed, attended)


def solution(mesh):
    split = P(("dp", "ctx"), None)
    in_specs = (
        split, split, split, P("dp", None), split, split, P(), P(), P(), P("dp"), split, split, split,
    )
    return jax.shard_map(
        on_device, mesh=mesh, in_specs=in_specs, out_specs=(split, split), check_vma=False
    )
```

```python
import functools

import jax
import jax.numpy as jnp
from jax import lax
from jax.experimental import pallas as pl
from jax.experimental.pallas import tpu as pltpu
from jax.sharding import PartitionSpec as P

F32 = jnp.float32
BF16 = jnp.bfloat16
MESH = pl.DeviceIdType.MESH
LOG2E = 1.4426950408889634
LN2 = 0.6931471805599453

ROWS = 128
CH = 4096
NS = 16
PLANES = 4
RING = 16
ZN = 8
HD = 128
GROUP = 4
STEPS = 16
HUGE = 3e38
MASKED = -1e30
RING_EVERY = 1
RING_TURNS = (
    (3, 1, 0), (4, 1, 1), (6, 2, 0), (8, 2, 1), (9, 1, 2), (10, 3, 0), (11, 1, 3), (13, 2, 2), (14, 3, 1), (15, 2, 3)
)
RING_OWN = ((4, 2), (7, 3))
RING_END = 14
STORES = 4
OWN = CH // RING
SCALE = LOG2E / HD**0.5
ROW_CONTRACT = (((0,), (0,)), ((), ()))
LANE_CONTRACT = (((1,), (1,)), ((), ()))


def iota(shape, dim):
    return lax.broadcasted_iota(jnp.int32, shape, dim)


def tree_sum(terms):
    while len(terms) > 1:
        terms = [a + b for a, b in zip(terms[::2], terms[1::2])]
    return terms[0]


def silu(v):
    return (0.5 * v) * (1.0 + jnp.tanh(0.5 * v))


def kernel(
    x_hbm, gate_hbm, step_hbm, decay_ref, in_ref, out_map_ref, taps_ref, bias_ref, skip_ref, seg_ref,
    q_hbm, k_hbm, v_hbm,
    mixed_hbm, attended_hbm,
    xv, gv, sv, halo, u_ref, s_ref, cum_ref, gs_ref, y_ref, ends_ref, rates_t, bb_ref, cc_ref,
    masks_ref, bias_row, kv, docs, q_in, q_aug, o_buf, m_out, lengths, plane_len, totals, plane_in, plane_total, across_in, entered, spread, entering,
    own_prefix,
    load_sem, halo_sem, qkv_send, qkv_recv, fwd_send, fwd_recv, bwd_send, bwd_recv, sib_send, sib_recv,
    len_send, len_recv, tot_send, tot_recv, acr_send, acr_recv, spr_send, spr_recv, o_send, o_recv, own_sem, store_sem,
):
    dp = lax.axis_index("dp")
    me = lax.axis_index("ctx")
    plane = me // RING
    r = me % RING
    z = r // 2
    core = r % 2

    def at(p, rr):
        return (dp, p * RING + rr)

    def remote(src, dst, send, recv, target):
        return pltpu.make_async_remote_copy(
            src_ref=src, dst_ref=dst, send_sem=send, recv_sem=recv, device_id=target, device_id_type=MESH
        )

    loads = [
        pltpu.make_async_copy(x_hbm, xv, load_sem.at[0]),
        pltpu.make_async_copy(step_hbm, sv, load_sem.at[1]),
        pltpu.make_async_copy(gate_hbm, gv, load_sem.at[2]),
    ]
    for load in loads:
        load.start()

    barrier = pltpu.get_barrier_semaphore()

    @pl.loop(1, RING)
    def _(j):
        pl.semaphore_signal(barrier, inc=1, device_id=at(plane, (r + j) % RING), device_id_type=MESH)

    @pl.loop(1, PLANES)
    def _(j):
        pl.semaphore_signal(barrier, inc=1, device_id=at((plane + j) % PLANES, r), device_id_type=MESH)

    count = PLANES * RING
    pl.semaphore_signal(barrier, inc=1, device_id=(dp, (me + 1) % count), device_id_type=MESH)
    pl.semaphore_signal(barrier, inc=1, device_id=(dp, (me + count - 1) % count), device_id_type=MESH)
    unit = (iota((16, HD), 0) == iota((16, HD), 1)).astype(BF16)
    doc_ids = iota((16, ROWS), 0).astype(F32)

    @pl.loop(0, PLANES * RING // 8, unroll=True)
    def _(g):
        rows = seg_ref[pl.ds(pl.multiple_of(g * 8, 8), 8), :].astype(F32)
        for i in range(8):
            hot = (doc_ids == rows[i : i + 1]).astype(BF16)
            cols = lax.dot_general(hot, unit, ROW_CONTRACT, preferred_element_type=F32)
            docs[g // 2, (g % 2) * 8 + i] = cols.astype(BF16)

    pl.semaphore_wait(barrier, RING - 1 + PLANES - 1 + 2)

    halo_copy = remote(
        x_hbm.at[pl.ds(ROWS - 16, 16), :], halo, halo_sem.at[0], halo_sem.at[1], (dp, (me + 1) % count)
    )
    halo_copy.start()

    def qkv_parts(p):
        return [
            (k_hbm.at[:, pl.ds(pl.multiple_of(p * HD, HD), HD)], kv.at[r, plane, :, pl.ds(0, HD)]),
            (v_hbm.at[:, pl.ds(pl.multiple_of(p * HD, HD), HD)], kv.at[r, plane, :, pl.ds(HD, HD)]),
            (q_hbm.at[:, pl.ds(pl.multiple_of(p * GROUP * HD, HD), GROUP * HD)], q_in.at[plane]),
        ]

    def qkv_copies(o, parts=(0, 1, 2)):
        p = (plane + o) % PLANES
        pairs = qkv_parts(p)
        return [
            remote(pairs[i][0], pairs[i][1], qkv_send.at[o, i], qkv_recv.at[o, i], at(p, r)) for i in parts
        ]

    for o in range(1, PLANES):
        for copy in qkv_copies(o, (0, 1)):
            copy.start()
    own_qkv = [pltpu.make_async_copy(s, d, own_sem.at[i]) for i, (s, d) in enumerate(qkv_parts(plane))]
    for copy in own_qkv:
        copy.start()

    p_ids, t_ids = iota((ROWS, ROWS), 0), iota((ROWS, ROWS), 1)
    perm = (t_ids == (p_ids % 8) * STEPS + p_ids // 8).astype(F32)
    perm_b = perm.astype(BF16)
    ones = jnp.ones((ROWS, ROWS), BF16)

    seg = seg_ref[...].astype(F32)
    block_ids = iota((PLANES * RING, ROWS), 0)

    def seg_row(b):
        return jnp.sum(jnp.where(block_ids == b, seg, 0.0), axis=0, keepdims=True)

    here = jnp.broadcast_to(seg_row(me), (8, ROWS))
    before = jnp.broadcast_to(jnp.where(me > 0, seg_row(me - 1), -1.0), (8, ROWS))
    lane8 = iota((8, ROWS), 1)
    for d in range(1, 4):
        ids = jnp.where(lane8 >= d, pltpu.roll(here, d, 1), pltpu.roll(before, d, 1))
        same = (ids == here).astype(F32)
        masks_ref[d] = jnp.dot((perm * same[0:1]).astype(BF16), ones, preferred_element_type=F32)
        if d == 1:
            fresh = ((ids != here) & (ids >= 0.0)).astype(F32)
            masks_ref[0] = jnp.dot((perm * fresh[0:1]).astype(BF16), ones, preferred_element_type=F32)

    repeat = (iota((NS, NS * 128), 0) == iota((NS, NS * 128), 1) // 128).astype(BF16)
    for src, dst in ((in_ref, bb_ref), (out_map_ref, cc_ref)):
        ordered = lax.dot_general(src[...], perm_b, LANE_CONTRACT, preferred_element_type=F32).astype(BF16)
        dst[...] = lax.dot_general(ordered, repeat, ROW_CONTRACT, preferred_element_type=F32)

    bias = bias_ref[...].astype(F32)
    for i in range(CH // 128):
        bias_row[:, pl.ds(i * 128, 128)] = bias[i : i + 1]

    rates_t[...] = jnp.minimum(decay_ref[...], -1e-30) * LOG2E

    def rate_rows(n, lanes):
        return jnp.broadcast_to(rates_t[pl.ds(n, 1), lanes], (8, 128))

    for p in range(PLANES):
        ids = seg_row(p * RING + r)
        cold = jnp.where((doc_ids != ids) & (doc_ids < 4.0), MASKED, 0.0).astype(BF16)
        cols = lax.dot_general(cold, unit, ROW_CONTRACT, preferred_element_type=F32).astype(BF16)
        for h in range(GROUP):
            q_aug[p, pl.ds(h * ROWS, ROWS), pl.ds(0, HD)] = cols

    def own_lanes(rr):
        return pl.ds(pl.multiple_of(rr * OWN, OWN), OWN)

    def lengths_copy(j):
        rr = (r + j) % RING
        return remote(lengths.at[:, own_lanes(rr)], plane_len.at[r], len_send.at[j], len_recv.at[j], at(plane, rr))

    def piece(rr, c):
        return kv.at[rr, c]

    def fwd(s, c):
        ref = piece(2 * ((z + ZN - s + 1) % ZN) + core, c)
        return remote(ref, ref, fwd_send.at[s, c], fwd_recv.at[s, c], at(plane, 2 * ((z + 1) % ZN) + core))

    def bwd(s, c):
        ref = piece(2 * ((z + s - 1) % ZN) + core, c)
        return remote(ref, ref, bwd_send.at[s, c], bwd_recv.at[s, c], at(plane, 2 * ((z + ZN - 1) % ZN) + core))

    def sibling(s, c):
        ref = piece(2 * ((z + ZN - s) % ZN) + core, c)
        return remote(ref, ref, sib_send.at[s, c], sib_recv.at[s, c], at(plane, 2 * z + 1 - core))

    def ring(s, c):
        return ([fwd(s, c)] if s < 4 or c < 2 else []) + ([bwd(s, c)] if s < 4 or c >= 2 else [])

    def own_piece(c):
        for copy in ring(1, c):
            copy.start()

    def ring_first():
        for copy in own_qkv[:2]:
            copy.wait()
        for o in range(1, PLANES):
            for copy in qkv_copies(o, (0, 1)):
                copy.wait_recv()
        for c in (0, 1):
            own_piece(c)
        for c in range(PLANES):
            sibling(0, c).start()

    def ring_turn(s, c):
        fwd(s, c).wait_recv()
        bwd(s, c).wait_recv()

        @pl.when((s < 3) | (c < 2))
        def _():
            fwd(s + 1, c).start()

        @pl.when((s < 3) | (c >= 2))
        def _():
            bwd(s + 1, c).start()

        sibling(s, c).start()
        sibling(ZN - s, c).start()

    def ring_last(c):
        for copy in ring(4, c):
            copy.wait_recv()
        sibling(4, c).start()

    def shared(c):
        for s in range(ZN):
            sibling(s, c).wait_recv()

    for load in loads:
        load.wait()
    W = 2048

    @pl.loop(0, CH // W)
    def _(b):
        lanes = pl.ds(pl.multiple_of(b * W, W), W)
        sp = jnp.dot(perm_b, sv[:, lanes], preferred_element_type=F32)
        gp = jnp.dot(perm_b, gv[:, lanes], preferred_element_type=F32)
        fresh = jnp.concatenate([masks_ref[0]] * (W // 128), axis=1)
        steps = jnp.where(fresh > 0.0, HUGE, sp)
        s_ref[:, lanes] = steps
        running = steps[0:8]
        cum_ref[pl.ds(0, 8), lanes] = running
        for i in range(1, STEPS):
            running = running + steps[i * 8 : i * 8 + 8]
            cum_ref[pl.ds(i * 8, 8), lanes] = running
        gs_ref[:, lanes] = silu(gp)
        for by in (1, 2, 4):
            running = running + jnp.where(iota((8, W), 0) >= by, pltpu.roll(running, by, 0), 0.0)
        lengths[:, lanes] = running[7:8]

    halo_copy.wait()

    @pl.loop(0, CH // W)
    def _(b):
        lanes = pl.ds(pl.multiple_of(b * W, W), W)
        xp = jnp.dot(perm_b, xv[:, lanes], preferred_element_type=F32)
        edge = halo[:, lanes].astype(F32)
        first = iota((8, W), 0) == 0
        lead = []
        for d in (3, 2, 1):
            rolled = pltpu.roll(xp[(STEPS - d) * 8 : (STEPS - d + 1) * 8], 1, 0)
            lead.append(jnp.where(first, edge[16 - d : 17 - d], rolled))
        extended = jnp.concatenate(lead + [xp], axis=0)
        taps = taps_ref[:, lanes].astype(F32)
        summed = bias_row[:, lanes] + taps[3:4] * xp
        for d in range(1, 4):
            allowed = jnp.concatenate([masks_ref[d]] * (W // 128), axis=1)
            earlier = extended[(3 - d) * 8 : (3 - d) * 8 + ROWS]
            summed = summed + taps[3 - d : 4 - d] * earlier * allowed
        u_ref[:, lanes] = silu(summed).astype(BF16).astype(F32)

    ring_first()
    for o in range(1, PLANES):
        for copy in qkv_copies(o, (2,)):
            copy.start()

    @pl.loop(1, RING)
    def _(j):
        lengths_copy(j).start()

    plane_len[r] = lengths[:, own_lanes(r)]

    sub = iota((8, 128), 0)

    def prefix_parts(lanes):
        total = cum_ref[pl.ds((STEPS - 1) * 8, 8), lanes]
        two = total + pltpu.roll(total, 1, 0)
        four = two + pltpu.roll(two, 2, 0)
        return total, two, four

    def scan(pair):
        blocks = [pl.ds(pl.multiple_of(pair * 256 + b * 128, 128), 128) for b in range(2)]
        spans = []
        for lanes in blocks:
            total, two, four = prefix_parts(lanes)
            spans.append([
                (1, jnp.where(sub >= 1, total, HUGE)),
                (2, jnp.where(sub >= 2, two, HUGE)),
                (4, jnp.where(sub >= 4, four, HUGE)),
            ])
        for first in range(0, NS, NS // 2):
            held_states = range(first, first + NS // 2)
            rates = [[rate_rows(n, lanes) for n in held_states] for lanes in blocks]
            states = [[jnp.zeros((8, 128), F32) for n in held_states] for lanes in blocks]
            for i in range(STEPS):
                rows = pl.ds(i * 8, 8)
                steps = [s_ref[rows, lanes] for lanes in blocks]
                drives = [u_ref[rows, lanes] for lanes in blocks]
                reads = [[], []]
                for k, n in enumerate(held_states):
                    into = bb_ref[rows, pl.ds(n * 128, 128)]
                    out_of = cc_ref[rows, pl.ds(n * 128, 128)]
                    for b in range(2):
                        exponent = steps[b] * rates[b][k]
                        factor = jnp.exp2(exponent)
                        ratio = jnp.tanh(exponent * (-0.5 * LN2))
                        part = ratio * lax.rsqrt(ratio) * (drives[b] * into)
                        states[b][k] = factor * (states[b][k] + part) + part
                        reads[b].append(out_of * states[b][k])
                for b, lanes in enumerate(blocks):
                    readout = tree_sum(reads[b])
                    y_ref[rows, lanes] = readout if first == 0 else y_ref[rows, lanes] + readout
            for b, lanes in enumerate(blocks):
                for k, n in enumerate(held_states):
                    state = states[b][k]
                    for by, span in spans[b]:
                        state = state + jnp.exp2(rates[b][k] * span) * pltpu.roll(state, by, 0)
                    totals[pl.ds(n, 1), lanes] = state[7:8]
                    ends_ref[n, :, lanes] = jnp.where(sub >= 1, pltpu.roll(state, 1, 0), 0.0)

    @pl.loop(0, CH // 256 // RING_EVERY)
    def _(group):
        code = sum(jnp.where(group == look, s * PLANES + c, 0) for look, s, c in RING_TURNS)

        @pl.when(code > 0)
        def _():
            ring_turn(code // PLANES, code % PLANES)

        for look, c in RING_OWN:
            @pl.when(group == look)
            def _():
                own_piece(c)

        @pl.when(group == RING_END)
        def _():
            ring_last(0)

        pl.loop(group * RING_EVERY, (group + 1) * RING_EVERY)(scan)

    def totals_copy(j):
        rr = (r + j) % RING
        return remote(totals.at[:, own_lanes(rr)], plane_in.at[r], tot_send.at[j], tot_recv.at[j], at(plane, rr))

    @pl.loop(1, RING)
    def _(j):
        totals_copy(j).start()

    plane_in[r] = totals[:, own_lanes(r)]

    for copy in own_qkv[2:]:
        copy.wait()
    for o in range(1, PLANES):
        for copy in qkv_copies(o, (2,)):
            copy.wait_recv()
    for p in range(PLANES):
        for h in range(GROUP):
            q_aug[p, pl.ds(h * ROWS, ROWS), pl.ds(HD, HD)] = q_in[p, :, pl.ds(h * HD, HD)]
    shared(0)

    CK = RING * ROWS

    def out_copy(p):
        return remote(
            o_buf.at[p],
            attended_hbm.at[:, pl.ds(pl.multiple_of(plane * GROUP * HD, HD), GROUP * HD)],
            o_send.at[p],
            o_recv.at[plane],
            at(p, r),
        )

    def own_out_copy(p):
        return pltpu.make_async_copy(
            o_buf.at[p],
            attended_hbm.at[:, pl.ds(pl.multiple_of(plane * GROUP * HD, HD), GROUP * HD)],
            own_sem.at[3],
        )

    def step_scores(p, c):
        keys = kv[:, c, :, pl.ds(0, HD)].reshape(CK, HD)
        keys = jnp.concatenate([docs[c].reshape(CK, HD), keys], axis=1)
        scores = lax.dot_general(keys, q_aug[p], LANE_CONTRACT, preferred_element_type=F32)
        if c == p:
            limit = iota((CK, GROUP * ROWS), 1) % ROWS + r * ROWS
            scores = jnp.where(iota((CK, GROUP * ROWS), 0) <= limit, scores, MASKED)
        return scores

    held = {}

    def step_rest(p, c, scores):
        values = kv[:, c, :, pl.ds(HD, HD)].reshape(CK, HD)
        top = jnp.max(scores, axis=0, keepdims=True) * SCALE
        if c > 0:
            old_top, old_acc, old_total = held[p]
            top = jnp.maximum(old_top, top)
        probs = jnp.exp2(scores * SCALE - top)
        total = jnp.sum(probs, axis=0, keepdims=True)
        acc = lax.dot_general(values, probs.astype(BF16), ROW_CONTRACT, preferred_element_type=F32)
        if c > 0:
            shrink = jnp.exp2(old_top - top)
            acc, total = old_acc * shrink + acc, old_total * shrink + total
        held[p] = top, acc, total
        if c < p:
            return
        result = acc / total
        for h in range(GROUP):
            o_buf[p, :, pl.ds(h * HD, HD)] = result[:, h * ROWS : (h + 1) * ROWS].T.astype(BF16)

        @pl.when(plane != p)
        def _():
            out_copy(p).start()

        @pl.when(plane == p)
        def _():
            own_out_copy(p).start()

    order = [(0, 0), (1, 0), (2, 0), (3, 0), (1, 1), (2, 1), (3, 1), (2, 2), (3, 2), (3, 3)]
    ahead = [step_scores(*order[0])]

    def attend(first, end):
        for k in range(first, end):
            scores = ahead.pop()
            if k + 1 < len(order):
                ahead.append(step_scores(*order[k + 1]))
            step_rest(*order[k], scores)

    attend(0, 1)
    ring_turn(3, 2)
    attend(1, 2)
    ring_last(1)
    ring_turn(3, 3)
    attend(2, 3)

    @pl.loop(1, RING)
    def _(j):
        totals_copy(j).wait_recv()
        lengths_copy(j).wait_recv()

    own_rates = rates_t[:, own_lanes(r)]
    state = jnp.zeros((NS, OWN), F32)
    length = jnp.zeros((1, OWN), F32)
    for i in range(RING):
        own_prefix[i, pl.ds(0, NS), :] = state
        own_prefix[i, pl.ds(NS, 8), :] = jnp.broadcast_to(length, (8, OWN))
        step = plane_len[i]
        state = jnp.exp2(own_rates * step) * state + plane_in[i]
        length = length + step
    plane_total[pl.ds(0, NS), :] = state
    plane_total[pl.ds(NS, 8), :] = jnp.broadcast_to(length, (8, OWN))

    def across_copy(o):
        p = (plane + o) % PLANES
        return remote(plane_total, across_in.at[plane], acr_send.at[o], acr_recv.at[o], at(p, r))

    for o in range(1, PLANES):
        across_copy(o).start()

    shared(1)
    attend(3, 4)
    ring_last(2)
    attend(4, 5)
    ring_last(3)
    attend(5, 6)
    shared(2)

    for o in range(1, PLANES):
        @pl.when(o <= plane)
        def _():
            across_copy(o).wait_recv()

    entered[...] = jnp.zeros((NS, OWN), F32)
    for p in range(PLANES - 1):
        @pl.when(p < plane)
        def _():
            moved = jnp.exp2(own_rates * across_in[p, pl.ds(NS, 1), :]) * entered[...]
            entered[...] = moved + across_in[p, pl.ds(0, NS), :]

    state = entered[...]
    for i in range(RING):
        moved = own_prefix[i, pl.ds(0, NS), :] + jnp.exp2(own_rates * own_prefix[i, pl.ds(NS, 1), :]) * state
        spread[i] = moved.astype(BF16)

    def spread_copy(j):
        rr = (r + j) % RING
        return remote(spread.at[rr], entering.at[:, own_lanes(r)], spr_send.at[j], spr_recv.at[j], at(plane, rr))

    @pl.loop(1, RING)
    def _(j):
        spread_copy(j).start()

    entering[:, own_lanes(r)] = spread[r]

    attend(6, 8)
    shared(3)
    attend(8, 10)

    @pl.loop(1, RING)
    def _(j):
        spread_copy(j).wait_recv()

    def store(s):
        lanes = pl.ds(s * (CH // STORES), CH // STORES)
        return pltpu.make_async_copy(m_out.at[:, lanes], mixed_hbm.at[:, lanes], store_sem.at[s])

    def finish(pair):
        blocks = [pl.ds(pl.multiple_of(pair * 256 + b * 128, 128), 128) for b in range(2)]
        leads, arriving = [], []
        for lanes in blocks:
            summed, _, _ = prefix_parts(lanes)
            for by in (1, 2, 4):
                summed = summed + jnp.where(sub >= by, pltpu.roll(summed, by, 0), 0.0)
            leads.append(jnp.where(sub >= 1, pltpu.roll(summed, 1, 0), 0.0))
            arriving.append(entering[:, lanes].astype(F32))
        for first in range(0, NS, NS // 2):
            held_states = range(first, first + NS // 2)
            rates = [[rate_rows(n, lanes) for n in held_states] for lanes in blocks]
            states = [
                [
                    jnp.exp2(rates[b][k] * leads[b]) * arriving[b][n : n + 1] + ends_ref[n, :, lanes]
                    for k, n in enumerate(held_states)
                ]
                for b, lanes in enumerate(blocks)
            ]
            for i in range(STEPS):
                rows = pl.ds(i * 8, 8)
                since = [cum_ref[rows, lanes] for lanes in blocks]
                reads = [[], []]
                for k, n in enumerate(held_states):
                    out_of = cc_ref[rows, pl.ds(n * 128, 128)]
                    for b in range(2):
                        reads[b].append(out_of * (jnp.exp2(since[b] * rates[b][k]) * states[b][k]))
                for b, lanes in enumerate(blocks):
                    readout = y_ref[rows, lanes] + tree_sum(reads[b])
                    if first == 0:
                        y_ref[rows, lanes] = readout
                    else:
                        direct = skip_ref[:, lanes] * u_ref[rows, lanes]
                        s_ref[rows, lanes] = (readout + direct) * gs_ref[rows, lanes]

    back = (p_ids == (t_ids % 8) * STEPS + t_ids // 8).astype(BF16)
    for s in range(STORES):
        pl.loop(s * (CH // 256 // STORES), (s + 1) * (CH // 256 // STORES))(finish)
        lanes = pl.ds(s * (CH // STORES), CH // STORES)
        m_out[:, lanes] = jnp.dot(back, s_ref[:, lanes].astype(BF16), preferred_element_type=F32).astype(BF16)
        store(s).start()

    for o in range(1, PLANES):
        for copy in qkv_copies(o):
            copy.wait_send()
        across_copy(o).wait_send()

        @pl.when(o > plane)
        def _():
            across_copy(o).wait_recv()

    for c in range(PLANES):
        for s in range(1, 5):
            for copy in ring(s, c):
                copy.wait_send()
        for s in range(ZN):
            sibling(s, c).wait_send()

    @pl.loop(1, RING)
    def _(j):
        totals_copy(j).wait_send()
        lengths_copy(j).wait_send()
        spread_copy(j).wait_send()

    for p in range(PLANES):
        @pl.when(plane != p)
        def _():
            out_copy(p).wait_send()
            pltpu.make_async_remote_copy(
                src_ref=o_buf.at[p],
                dst_ref=attended_hbm.at[:, pl.ds(p * GROUP * HD, GROUP * HD)],
                send_sem=o_send.at[p],
                recv_sem=o_recv.at[p],
                device_id=at(p, r),
                device_id_type=MESH,
            ).wait_recv()

        @pl.when(plane == p)
        def _():
            own_out_copy(p).wait()

    for s in range(STORES):
        store(s).wait()


def hand_over(mixed, attended, mixed_out, attended_out, mixed_buf, attended_buf, sem):
    inward, outward = [], []
    for src, buf, dst, pieces in ((mixed, mixed_buf, mixed_out, 4), (attended, attended_buf, attended_out, 2)):
        for i in range(pieces):
            lanes = pl.ds(i * 1024, 1024)
            inward.append(pltpu.make_async_copy(src.at[:, lanes], buf.at[:, lanes], sem.at[0, len(inward)]))
            outward.append(pltpu.make_async_copy(buf.at[:, lanes], dst.at[:, lanes], sem.at[1, len(outward)]))
    for copy in inward:
        copy.start()
    for arrival, copy in zip(inward, outward):
        arrival.wait()
        copy.start()
    for copy in outward:
        copy.wait()


def on_device(
    mamba_input, gate_branch, step_size, decay_rates, input_map, output_map, mixing_weight, mixing_bias,
    skip_gain, segments, query_rows, key_rows, value_rows,
):
    hbm = pl.BlockSpec(memory_space=pl.ANY)
    vmem = pl.BlockSpec(memory_space=pltpu.VMEM)
    big = pltpu.VMEM((ROWS, CH), F32)
    dma = pltpu.SemaphoreType.DMA
    mixed, attended = pl.pallas_call(
        kernel,
        out_shape=(
            jax.ShapeDtypeStruct((ROWS, CH), BF16),
            jax.ShapeDtypeStruct((ROWS, PLANES * GROUP * HD), BF16),
        ),
        in_specs=[hbm] * 3 + [vmem] * 7 + [hbm] * 3,
        out_specs=(hbm, hbm),
        scratch_shapes=[
            pltpu.VMEM((ROWS, CH), BF16),
            pltpu.VMEM((ROWS, CH), BF16),
            pltpu.VMEM((ROWS, CH), BF16),
            pltpu.VMEM((16, CH), BF16),
            big, big, big, big, big,
            pltpu.VMEM((NS, 8, CH), F32),
            pltpu.VMEM((NS, CH), F32),
            pltpu.VMEM((ROWS, NS * 128), F32),
            pltpu.VMEM((ROWS, NS * 128), F32),
            pltpu.VMEM((4, ROWS, ROWS), F32),
            pltpu.VMEM((1, CH), F32),
            pltpu.VMEM((RING, PLANES, ROWS, 2 * HD), BF16),
            pltpu.VMEM((PLANES, RING, ROWS, HD), BF16),
            pltpu.VMEM((PLANES, ROWS, GROUP * HD), BF16),
            pltpu.VMEM((PLANES, GROUP * ROWS, 2 * HD), BF16),
            pltpu.VMEM((PLANES, ROWS, GROUP * HD), BF16),
            pltpu.VMEM((ROWS, CH), BF16),
            pltpu.VMEM((1, CH), F32),
            pltpu.VMEM((RING, 1, OWN), F32),
            pltpu.VMEM((NS, CH), F32),
            pltpu.VMEM((RING, NS, OWN), F32),
            pltpu.VMEM((NS + 8, OWN), F32),
            pltpu.VMEM((PLANES, NS + 8, OWN), F32),
            pltpu.VMEM((NS, OWN), F32),
            pltpu.VMEM((RING, NS, OWN), BF16),
            pltpu.VMEM((NS, CH), BF16),
            pltpu.VMEM((RING, NS + 8, OWN), F32),
            dma((3,)), dma((2,)), dma((4, 3)), dma((4, 3)),
            dma((5, 4)), dma((5, 4)), dma((5, 4)), dma((5, 4)), dma((ZN, 4)), dma((ZN, 4)),
            dma((RING,)), dma((RING,)), dma((RING,)), dma((RING,)), dma((PLANES,)), dma((PLANES,)), dma((RING,)), dma((RING,)),
            dma((PLANES,)), dma((PLANES,)), dma((4,)), dma((STORES,)),
        ],
        compiler_params=pltpu.CompilerParams(
            collective_id=0, has_side_effects=True, vmem_limit_bytes=60 * 2**20
        ),
        name="mixer",
    )(
        mamba_input, gate_branch, step_size, decay_rates.T, input_map.T, output_map.T, mixing_weight,
        mixing_bias.reshape(CH // 128, 128), skip_gain.reshape(1, CH), segments.reshape(PLANES * RING, ROWS),
        query_rows, key_rows, value_rows,
    )
    shapes = (jax.ShapeDtypeStruct(mixed.shape, BF16), jax.ShapeDtypeStruct(attended.shape, BF16))
    return pl.pallas_call(
        hand_over,
        out_shape=shapes,
        in_specs=[hbm] * 2,
        out_specs=(hbm, hbm),
        scratch_shapes=[
            pltpu.VMEM(mixed.shape, BF16), pltpu.VMEM(attended.shape, BF16), dma((2, 6)),
        ],
        compiler_params=pltpu.CompilerParams(vmem_limit_bytes=60 * 2**20),
        name="hand_over",
    )(mixed, attended)


def solution(mesh):
    split = P(("dp", "ctx"), None)
    in_specs = (
        split, split, split, P("dp", None), split, split, P(), P(), P(), P("dp"), split, split, split,
    )
    return jax.shard_map(
        on_device, mesh=mesh, in_specs=in_specs, out_specs=(split, split), check_vma=False
    )
```

```python
import functools

import jax
import jax.numpy as jnp
from jax import lax
from jax.experimental import pallas as pl
from jax.experimental.pallas import tpu as pltpu
from jax.sharding import PartitionSpec as P

F32 = jnp.float32
BF16 = jnp.bfloat16
MESH = pl.DeviceIdType.MESH
LOG2E = 1.4426950408889634
LN2 = 0.6931471805599453

ROWS = 128
CH = 4096
NS = 16
PLANES = 4
RING = 16
ZN = 8
HD = 128
GROUP = 4
STEPS = 16
HUGE = 3e38
MASKED = -1e30
RING_EVERY = 1
RING_TURNS = (
    (3, 1, 0), (4, 1, 1), (6, 2, 0), (8, 2, 1), (9, 1, 2), (10, 3, 0), (11, 1, 3), (13, 2, 2), (14, 3, 1), (15, 2, 3)
)
RING_OWN = ((4, 2), (7, 3))
RING_END = 14
RING_REST = 5
STORES = 4
OWN = CH // RING
SCALE = LOG2E / HD**0.5
ROW_CONTRACT = (((0,), (0,)), ((), ()))
LANE_CONTRACT = (((1,), (1,)), ((), ()))


def iota(shape, dim):
    return lax.broadcasted_iota(jnp.int32, shape, dim)


def tree_sum(terms):
    while len(terms) > 1:
        terms = [a + b for a, b in zip(terms[::2], terms[1::2])]
    return terms[0]


def silu(v):
    return (0.5 * v) * (1.0 + jnp.tanh(0.5 * v))


def kernel(
    x_hbm, gate_hbm, step_hbm, decay_ref, in_ref, out_map_ref, taps_ref, bias_ref, skip_ref, seg_ref,
    q_hbm, k_hbm, v_hbm,
    mixed_hbm, attended_hbm,
    xv, gv, sv, halo, u_ref, s_ref, cum_ref, gs_ref, y_ref, ends_ref, rates_t, bb_ref, cc_ref,
    masks_ref, bias_row, kv, docs, q_in, q_aug, o_buf, m_out, lengths, plane_len, totals, plane_in, plane_total, across_in, entered, spread, entering,
    own_prefix,
    load_sem, halo_sem, qkv_send, qkv_recv, fwd_send, fwd_recv, bwd_send, bwd_recv, sib_send, sib_recv,
    len_send, len_recv, tot_send, tot_recv, acr_send, acr_recv, spr_send, spr_recv, o_send, o_recv, own_sem, store_sem,
):
    dp = lax.axis_index("dp")
    me = lax.axis_index("ctx")
    plane = me // RING
    r = me % RING
    z = r // 2
    core = r % 2

    def at(p, rr):
        return (dp, p * RING + rr)

    def remote(src, dst, send, recv, target):
        return pltpu.make_async_remote_copy(
            src_ref=src, dst_ref=dst, send_sem=send, recv_sem=recv, device_id=target, device_id_type=MESH
        )

    loads = [
        pltpu.make_async_copy(x_hbm, xv, load_sem.at[0]),
        pltpu.make_async_copy(step_hbm, sv, load_sem.at[1]),
        pltpu.make_async_copy(gate_hbm, gv, load_sem.at[2]),
    ]
    for load in loads:
        load.start()

    barrier = pltpu.get_barrier_semaphore()

    @pl.loop(1, RING)
    def _(j):
        pl.semaphore_signal(barrier, inc=1, device_id=at(plane, (r + j) % RING), device_id_type=MESH)

    @pl.loop(1, PLANES)
    def _(j):
        pl.semaphore_signal(barrier, inc=1, device_id=at((plane + j) % PLANES, r), device_id_type=MESH)

    count = PLANES * RING
    pl.semaphore_signal(barrier, inc=1, device_id=(dp, (me + 1) % count), device_id_type=MESH)
    pl.semaphore_signal(barrier, inc=1, device_id=(dp, (me + count - 1) % count), device_id_type=MESH)
    unit = (iota((16, HD), 0) == iota((16, HD), 1)).astype(BF16)
    doc_ids = iota((16, ROWS), 0).astype(F32)

    @pl.loop(0, PLANES * RING // 8, unroll=True)
    def _(g):
        rows = seg_ref[pl.ds(pl.multiple_of(g * 8, 8), 8), :].astype(F32)
        for i in range(8):
            hot = (doc_ids == rows[i : i + 1]).astype(BF16)
            cols = lax.dot_general(hot, unit, ROW_CONTRACT, preferred_element_type=F32)
            docs[g // 2, (g % 2) * 8 + i] = cols.astype(BF16)

    pl.semaphore_wait(barrier, RING - 1 + PLANES - 1 + 2)

    halo_copy = remote(
        x_hbm.at[pl.ds(ROWS - 16, 16), :], halo, halo_sem.at[0], halo_sem.at[1], (dp, (me + 1) % count)
    )
    halo_copy.start()

    def qkv_parts(p):
        return [
            (k_hbm.at[:, pl.ds(pl.multiple_of(p * HD, HD), HD)], kv.at[r, plane, :, pl.ds(0, HD)]),
            (v_hbm.at[:, pl.ds(pl.multiple_of(p * HD, HD), HD)], kv.at[r, plane, :, pl.ds(HD, HD)]),
            (q_hbm.at[:, pl.ds(pl.multiple_of(p * GROUP * HD, HD), GROUP * HD)], q_in.at[plane]),
        ]

    def qkv_copies(o, parts=(0, 1, 2)):
        p = (plane + o) % PLANES
        pairs = qkv_parts(p)
        return [
            remote(pairs[i][0], pairs[i][1], qkv_send.at[o, i], qkv_recv.at[o, i], at(p, r)) for i in parts
        ]

    for o in range(1, PLANES):
        for copy in qkv_copies(o, (0, 1)):
            copy.start()
    own_qkv = [pltpu.make_async_copy(s, d, own_sem.at[i]) for i, (s, d) in enumerate(qkv_parts(plane))]
    for copy in own_qkv:
        copy.start()

    p_ids, t_ids = iota((ROWS, ROWS), 0), iota((ROWS, ROWS), 1)
    perm = (t_ids == (p_ids % 8) * STEPS + p_ids // 8).astype(F32)
    perm_b = perm.astype(BF16)
    ones = jnp.ones((ROWS, ROWS), BF16)

    seg = seg_ref[...].astype(F32)
    block_ids = iota((PLANES * RING, ROWS), 0)

    def seg_row(b):
        return jnp.sum(jnp.where(block_ids == b, seg, 0.0), axis=0, keepdims=True)

    here = jnp.broadcast_to(seg_row(me), (8, ROWS))
    before = jnp.broadcast_to(jnp.where(me > 0, seg_row(me - 1), -1.0), (8, ROWS))
    lane8 = iota((8, ROWS), 1)
    for d in range(1, 4):
        ids = jnp.where(lane8 >= d, pltpu.roll(here, d, 1), pltpu.roll(before, d, 1))
        same = (ids == here).astype(F32)
        masks_ref[d] = jnp.dot((perm * same[0:1]).astype(BF16), ones, preferred_element_type=F32)
        if d == 1:
            fresh = ((ids != here) & (ids >= 0.0)).astype(F32)
            masks_ref[0] = jnp.dot((perm * fresh[0:1]).astype(BF16), ones, preferred_element_type=F32)

    repeat = (iota((NS, NS * 128), 0) == iota((NS, NS * 128), 1) // 128).astype(BF16)
    for src, dst in ((in_ref, bb_ref), (out_map_ref, cc_ref)):
        ordered = lax.dot_general(src[...], perm_b, LANE_CONTRACT, preferred_element_type=F32).astype(BF16)
        dst[...] = lax.dot_general(ordered, repeat, ROW_CONTRACT, preferred_element_type=F32)

    bias = bias_ref[...].astype(F32)
    for i in range(CH // 128):
        bias_row[:, pl.ds(i * 128, 128)] = bias[i : i + 1]

    rates_t[...] = jnp.minimum(decay_ref[...], -1e-30) * LOG2E

    def rate_rows(n, lanes):
        return jnp.broadcast_to(rates_t[pl.ds(n, 1), lanes], (8, 128))

    for p in range(PLANES):
        ids = seg_row(p * RING + r)
        cold = jnp.where((doc_ids != ids) & (doc_ids < 4.0), MASKED, 0.0).astype(BF16)
        cols = lax.dot_general(cold, unit, ROW_CONTRACT, preferred_element_type=F32).astype(BF16)
        for h in range(GROUP):
            q_aug[p, pl.ds(h * ROWS, ROWS), pl.ds(0, HD)] = cols

    def own_lanes(rr):
        return pl.ds(pl.multiple_of(rr * OWN, OWN), OWN)

    def lengths_copy(j):
        rr = (r + j) % RING
        return remote(lengths.at[:, own_lanes(rr)], plane_len.at[r], len_send.at[j], len_recv.at[j], at(plane, rr))

    def piece(rr, c):
        return kv.at[rr, c]

    def fwd(s, c):
        ref = piece(2 * ((z + ZN - s + 1) % ZN) + core, c)
        return remote(ref, ref, fwd_send.at[s, c], fwd_recv.at[s, c], at(plane, 2 * ((z + 1) % ZN) + core))

    def bwd(s, c):
        ref = piece(2 * ((z + s - 1) % ZN) + core, c)
        return remote(ref, ref, bwd_send.at[s, c], bwd_recv.at[s, c], at(plane, 2 * ((z + ZN - 1) % ZN) + core))

    def sibling(s, c):
        ref = piece(2 * ((z + ZN - s) % ZN) + core, c)
        return remote(ref, ref, sib_send.at[s, c], sib_recv.at[s, c], at(plane, 2 * z + 1 - core))

    def ring(s, c):
        return ([fwd(s, c)] if s < 4 or c < 2 else []) + ([bwd(s, c)] if s < 4 or c >= 2 else [])

    def own_piece(c):
        for copy in ring(1, c):
            copy.start()

    def ring_first():
        for copy in own_qkv[:2]:
            copy.wait()
        for o in range(1, PLANES):
            for copy in qkv_copies(o, (0, 1)):
                copy.wait_recv()
        for c in (0, 1):
            own_piece(c)
        sibling(0, 0).start()

    def ring_turn(s, c):
        fwd(s, c).wait_recv()
        bwd(s, c).wait_recv()

        @pl.when((s < 3) | (c < 2))
        def _():
            fwd(s + 1, c).start()

        @pl.when((s < 3) | (c >= 2))
        def _():
            bwd(s + 1, c).start()

        sibling(s, c).start()
        sibling(ZN - s, c).start()

    def ring_last(c):
        for copy in ring(4, c):
            copy.wait_recv()
        sibling(4, c).start()

    def shared(c):
        for s in range(ZN):
            sibling(s, c).wait_recv()

    for load in loads:
        load.wait()
    W = 2048

    @pl.loop(0, CH // W)
    def _(b):
        lanes = pl.ds(pl.multiple_of(b * W, W), W)
        sp = jnp.dot(perm_b, sv[:, lanes], preferred_element_type=F32)
        gp = jnp.dot(perm_b, gv[:, lanes], preferred_element_type=F32)
        fresh = jnp.concatenate([masks_ref[0]] * (W // 128), axis=1)
        steps = jnp.where(fresh > 0.0, HUGE, sp)
        s_ref[:, lanes] = steps
        running = steps[0:8]
        cum_ref[pl.ds(0, 8), lanes] = running
        for i in range(1, STEPS):
            running = running + steps[i * 8 : i * 8 + 8]
            cum_ref[pl.ds(i * 8, 8), lanes] = running
        gs_ref[:, lanes] = silu(gp)
        for by in (1, 2, 4):
            running = running + jnp.where(iota((8, W), 0) >= by, pltpu.roll(running, by, 0), 0.0)
        lengths[:, lanes] = running[7:8]

    halo_copy.wait()

    @pl.loop(0, CH // W)
    def _(b):
        lanes = pl.ds(pl.multiple_of(b * W, W), W)
        xp = jnp.dot(perm_b, xv[:, lanes], preferred_element_type=F32)
        edge = halo[:, lanes].astype(F32)
        first = iota((8, W), 0) == 0
        lead = []
        for d in (3, 2, 1):
            rolled = pltpu.roll(xp[(STEPS - d) * 8 : (STEPS - d + 1) * 8], 1, 0)
            lead.append(jnp.where(first, edge[16 - d : 17 - d], rolled))
        extended = jnp.concatenate(lead + [xp], axis=0)
        taps = taps_ref[:, lanes].astype(F32)
        summed = bias_row[:, lanes] + taps[3:4] * xp
        for d in range(1, 4):
            allowed = jnp.concatenate([masks_ref[d]] * (W // 128), axis=1)
            earlier = extended[(3 - d) * 8 : (3 - d) * 8 + ROWS]
            summed = summed + taps[3 - d : 4 - d] * earlier * allowed
        u_ref[:, lanes] = silu(summed).astype(BF16).astype(F32)

    ring_first()
    @pl.loop(1, RING)
    def _(j):
        lengths_copy(j).start()

    plane_len[r] = lengths[:, own_lanes(r)]

    sub = iota((8, 128), 0)

    def prefix_parts(lanes):
        total = cum_ref[pl.ds((STEPS - 1) * 8, 8), lanes]
        two = total + pltpu.roll(total, 1, 0)
        four = two + pltpu.roll(two, 2, 0)
        return total, two, four

    def scan(pair):
        blocks = [pl.ds(pl.multiple_of(pair * 256 + b * 128, 128), 128) for b in range(2)]
        spans = []
        for lanes in blocks:
            total, two, four = prefix_parts(lanes)
            spans.append([
                (1, jnp.where(sub >= 1, total, HUGE)),
                (2, jnp.where(sub >= 2, two, HUGE)),
                (4, jnp.where(sub >= 4, four, HUGE)),
            ])
        for first in range(0, NS, NS // 2):
            held_states = range(first, first + NS // 2)
            rates = [[rate_rows(n, lanes) for n in held_states] for lanes in blocks]
            states = [[jnp.zeros((8, 128), F32) for n in held_states] for lanes in blocks]
            for i in range(STEPS):
                rows = pl.ds(i * 8, 8)
                steps = [s_ref[rows, lanes] for lanes in blocks]
                drives = [u_ref[rows, lanes] for lanes in blocks]
                reads = [[], []]
                for k, n in enumerate(held_states):
                    into = bb_ref[rows, pl.ds(n * 128, 128)]
                    out_of = cc_ref[rows, pl.ds(n * 128, 128)]
                    for b in range(2):
                        exponent = steps[b] * rates[b][k]
                        factor = jnp.exp2(exponent)
                        ratio = jnp.tanh(exponent * (-0.5 * LN2))
                        part = ratio * lax.rsqrt(ratio) * (drives[b] * into)
                        states[b][k] = factor * (states[b][k] + part) + part
                        reads[b].append(out_of * states[b][k])
                for b, lanes in enumerate(blocks):
                    readout = tree_sum(reads[b])
                    y_ref[rows, lanes] = readout if first == 0 else y_ref[rows, lanes] + readout
            for b, lanes in enumerate(blocks):
                for k, n in enumerate(held_states):
                    state = states[b][k]
                    for by, span in spans[b]:
                        state = state + jnp.exp2(rates[b][k] * span) * pltpu.roll(state, by, 0)
                    totals[pl.ds(n, 1), lanes] = state[7:8]
                    ends_ref[n, :, lanes] = jnp.where(sub >= 1, pltpu.roll(state, 1, 0), 0.0)

    @pl.loop(0, CH // 256 // RING_EVERY)
    def _(group):
        code = sum(jnp.where(group == look, s * PLANES + c, 0) for look, s, c in RING_TURNS)

        @pl.when(code > 0)
        def _():
            ring_turn(code // PLANES, code % PLANES)

        for look, c in RING_OWN:
            @pl.when(group == look)
            def _():
                own_piece(c)

        @pl.when(group == RING_REST)
        def _():
            for c in range(1, PLANES):
                sibling(0, c).start()
            for o in range(1, PLANES):
                for copy in qkv_copies(o, (2,)):
                    copy.start()

        @pl.when(group == RING_END)
        def _():
            ring_last(0)

        pl.loop(group * RING_EVERY, (group + 1) * RING_EVERY)(scan)

    def totals_copy(j):
        rr = (r + j) % RING
        return remote(totals.at[:, own_lanes(rr)], plane_in.at[r], tot_send.at[j], tot_recv.at[j], at(plane, rr))

    @pl.loop(1, RING)
    def _(j):
        totals_copy(j).start()

    plane_in[r] = totals[:, own_lanes(r)]

    for copy in own_qkv[2:]:
        copy.wait()
    for o in range(1, PLANES):
        for copy in qkv_copies(o, (2,)):
            copy.wait_recv()
    for p in range(PLANES):
        for h in range(GROUP):
            q_aug[p, pl.ds(h * ROWS, ROWS), pl.ds(HD, HD)] = q_in[p, :, pl.ds(h * HD, HD)]
    shared(0)

    CK = RING * ROWS

    def out_copy(p):
        return remote(
            o_buf.at[p],
            attended_hbm.at[:, pl.ds(pl.multiple_of(plane * GROUP * HD, HD), GROUP * HD)],
            o_send.at[p],
            o_recv.at[plane],
            at(p, r),
        )

    def own_out_copy(p):
        return pltpu.make_async_copy(
            o_buf.at[p],
            attended_hbm.at[:, pl.ds(pl.multiple_of(plane * GROUP * HD, HD), GROUP * HD)],
            own_sem.at[3],
        )

    def step_scores(p, c):
        keys = kv[:, c, :, pl.ds(0, HD)].reshape(CK, HD)
        keys = jnp.concatenate([docs[c].reshape(CK, HD), keys], axis=1)
        scores = lax.dot_general(keys, q_aug[p], LANE_CONTRACT, preferred_element_type=F32)
        if c == p:
            limit = iota((CK, GROUP * ROWS), 1) % ROWS + r * ROWS
            scores = jnp.where(iota((CK, GROUP * ROWS), 0) <= limit, scores, MASKED)
        return scores

    held = {}

    def step_rest(p, c, scores):
        values = kv[:, c, :, pl.ds(HD, HD)].reshape(CK, HD)
        top = jnp.max(scores, axis=0, keepdims=True) * SCALE
        if c > 0:
            old_top, old_acc, old_total = held[p]
            top = jnp.maximum(old_top, top)
        probs = jnp.exp2(scores * SCALE - top)
        total = jnp.sum(probs, axis=0, keepdims=True)
        acc = lax.dot_general(values, probs.astype(BF16), ROW_CONTRACT, preferred_element_type=F32)
        if c > 0:
            shrink = jnp.exp2(old_top - top)
            acc, total = old_acc * shrink + acc, old_total * shrink + total
        held[p] = top, acc, total
        if c < p:
            return
        result = acc / total
        for h in range(GROUP):
            o_buf[p, :, pl.ds(h * HD, HD)] = result[:, h * ROWS : (h + 1) * ROWS].T.astype(BF16)

        @pl.when(plane != p)
        def _():
            out_copy(p).start()

        @pl.when(plane == p)
        def _():
            own_out_copy(p).start()

    order = [(0, 0), (1, 0), (2, 0), (3, 0), (1, 1), (2, 1), (3, 1), (2, 2), (3, 2), (3, 3)]
    ahead = [step_scores(*order[0])]

    def attend(first, end):
        for k in range(first, end):
            scores = ahead.pop()
            if k + 1 < len(order):
                ahead.append(step_scores(*order[k + 1]))
            step_rest(*order[k], scores)

    attend(0, 1)
    ring_turn(3, 2)
    attend(1, 2)
    ring_last(1)
    ring_turn(3, 3)
    attend(2, 3)

    @pl.loop(1, RING)
    def _(j):
        totals_copy(j).wait_recv()
        lengths_copy(j).wait_recv()

    own_rates = rates_t[:, own_lanes(r)]
    state = jnp.zeros((NS, OWN), F32)
    length = jnp.zeros((1, OWN), F32)
    for i in range(RING):
        own_prefix[i, pl.ds(0, NS), :] = state
        own_prefix[i, pl.ds(NS, 8), :] = jnp.broadcast_to(length, (8, OWN))
        step = plane_len[i]
        state = jnp.exp2(own_rates * step) * state + plane_in[i]
        length = length + step
    plane_total[pl.ds(0, NS), :] = state
    plane_total[pl.ds(NS, 8), :] = jnp.broadcast_to(length, (8, OWN))

    def across_copy(o):
        p = (plane + o) % PLANES
        return remote(plane_total, across_in.at[plane], acr_send.at[o], acr_recv.at[o], at(p, r))

    for o in range(1, PLANES):
        across_copy(o).start()

    shared(1)
    attend(3, 4)
    ring_last(2)
    attend(4, 5)
    ring_last(3)
    attend(5, 6)
    shared(2)

    for o in range(1, PLANES):
        @pl.when(o <= plane)
        def _():
            across_copy(o).wait_recv()

    entered[...] = jnp.zeros((NS, OWN), F32)
    for p in range(PLANES - 1):
        @pl.when(p < plane)
        def _():
            moved = jnp.exp2(own_rates * across_in[p, pl.ds(NS, 1), :]) * entered[...]
            entered[...] = moved + across_in[p, pl.ds(0, NS), :]

    state = entered[...]
    for i in range(RING):
        moved = own_prefix[i, pl.ds(0, NS), :] + jnp.exp2(own_rates * own_prefix[i, pl.ds(NS, 1), :]) * state
        spread[i] = moved.astype(BF16)

    def spread_copy(j):
        rr = (r + j) % RING
        return remote(spread.at[rr], entering.at[:, own_lanes(r)], spr_send.at[j], spr_recv.at[j], at(plane, rr))

    @pl.loop(1, RING)
    def _(j):
        spread_copy(j).start()

    entering[:, own_lanes(r)] = spread[r]

    attend(6, 8)
    shared(3)
    attend(8, 10)

    @pl.loop(1, RING)
    def _(j):
        spread_copy(j).wait_recv()

    def store(s):
        lanes = pl.ds(s * (CH // STORES), CH // STORES)
        return pltpu.make_async_copy(m_out.at[:, lanes], mixed_hbm.at[:, lanes], store_sem.at[s])

    def finish(pair):
        blocks = [pl.ds(pl.multiple_of(pair * 256 + b * 128, 128), 128) for b in range(2)]
        leads, arriving = [], []
        for lanes in blocks:
            summed, _, _ = prefix_parts(lanes)
            for by in (1, 2, 4):
                summed = summed + jnp.where(sub >= by, pltpu.roll(summed, by, 0), 0.0)
            leads.append(jnp.where(sub >= 1, pltpu.roll(summed, 1, 0), 0.0))
            arriving.append(entering[:, lanes].astype(F32))
        for first in range(0, NS, NS // 2):
            held_states = range(first, first + NS // 2)
            rates = [[rate_rows(n, lanes) for n in held_states] for lanes in blocks]
            states = [
                [
                    jnp.exp2(rates[b][k] * leads[b]) * arriving[b][n : n + 1] + ends_ref[n, :, lanes]
                    for k, n in enumerate(held_states)
                ]
                for b, lanes in enumerate(blocks)
            ]
            for i in range(STEPS):
                rows = pl.ds(i * 8, 8)
                since = [cum_ref[rows, lanes] for lanes in blocks]
                reads = [[], []]
                for k, n in enumerate(held_states):
                    out_of = cc_ref[rows, pl.ds(n * 128, 128)]
                    for b in range(2):
                        reads[b].append(out_of * (jnp.exp2(since[b] * rates[b][k]) * states[b][k]))
                for b, lanes in enumerate(blocks):
                    readout = y_ref[rows, lanes] + tree_sum(reads[b])
                    if first == 0:
                        y_ref[rows, lanes] = readout
                    else:
                        direct = skip_ref[:, lanes] * u_ref[rows, lanes]
                        s_ref[rows, lanes] = (readout + direct) * gs_ref[rows, lanes]

    back = (p_ids == (t_ids % 8) * STEPS + t_ids // 8).astype(BF16)
    for s in range(STORES):
        pl.loop(s * (CH // 256 // STORES), (s + 1) * (CH // 256 // STORES))(finish)
        lanes = pl.ds(s * (CH // STORES), CH // STORES)
        m_out[:, lanes] = jnp.dot(back, s_ref[:, lanes].astype(BF16), preferred_element_type=F32).astype(BF16)
        store(s).start()

    for o in range(1, PLANES):
        for copy in qkv_copies(o):
            copy.wait_send()
        across_copy(o).wait_send()

        @pl.when(o > plane)
        def _():
            across_copy(o).wait_recv()

    for c in range(PLANES):
        for s in range(1, 5):
            for copy in ring(s, c):
                copy.wait_send()
        for s in range(ZN):
            sibling(s, c).wait_send()

    @pl.loop(1, RING)
    def _(j):
        totals_copy(j).wait_send()
        lengths_copy(j).wait_send()
        spread_copy(j).wait_send()

    for p in range(PLANES):
        @pl.when(plane != p)
        def _():
            out_copy(p).wait_send()
            pltpu.make_async_remote_copy(
                src_ref=o_buf.at[p],
                dst_ref=attended_hbm.at[:, pl.ds(p * GROUP * HD, GROUP * HD)],
                send_sem=o_send.at[p],
                recv_sem=o_recv.at[p],
                device_id=at(p, r),
                device_id_type=MESH,
            ).wait_recv()

        @pl.when(plane == p)
        def _():
            own_out_copy(p).wait()

    for s in range(STORES):
        store(s).wait()


def hand_over(mixed, attended, mixed_out, attended_out, mixed_buf, attended_buf, sem):
    inward, outward = [], []
    for src, buf, dst, pieces in ((mixed, mixed_buf, mixed_out, 4), (attended, attended_buf, attended_out, 2)):
        for i in range(pieces):
            lanes = pl.ds(i * 1024, 1024)
            inward.append(pltpu.make_async_copy(src.at[:, lanes], buf.at[:, lanes], sem.at[0, len(inward)]))
            outward.append(pltpu.make_async_copy(buf.at[:, lanes], dst.at[:, lanes], sem.at[1, len(outward)]))
    for copy in inward:
        copy.start()
    for arrival, copy in zip(inward, outward):
        arrival.wait()
        copy.start()
    for copy in outward:
        copy.wait()


def on_device(
    mamba_input, gate_branch, step_size, decay_rates, input_map, output_map, mixing_weight, mixing_bias,
    skip_gain, segments, query_rows, key_rows, value_rows,
):
    hbm = pl.BlockSpec(memory_space=pl.ANY)
    vmem = pl.BlockSpec(memory_space=pltpu.VMEM)
    big = pltpu.VMEM((ROWS, CH), F32)
    dma = pltpu.SemaphoreType.DMA
    mixed, attended = pl.pallas_call(
        kernel,
        out_shape=(
            jax.ShapeDtypeStruct((ROWS, CH), BF16),
            jax.ShapeDtypeStruct((ROWS, PLANES * GROUP * HD), BF16),
        ),
        in_specs=[hbm] * 3 + [vmem] * 7 + [hbm] * 3,
        out_specs=(hbm, hbm),
        scratch_shapes=[
            pltpu.VMEM((ROWS, CH), BF16),
            pltpu.VMEM((ROWS, CH), BF16),
            pltpu.VMEM((ROWS, CH), BF16),
            pltpu.VMEM((16, CH), BF16),
            big, big, big, big, big,
            pltpu.VMEM((NS, 8, CH), F32),
            pltpu.VMEM((NS, CH), F32),
            pltpu.VMEM((ROWS, NS * 128), F32),
            pltpu.VMEM((ROWS, NS * 128), F32),
            pltpu.VMEM((4, ROWS, ROWS), F32),
            pltpu.VMEM((1, CH), F32),
            pltpu.VMEM((RING, PLANES, ROWS, 2 * HD), BF16),
            pltpu.VMEM((PLANES, RING, ROWS, HD), BF16),
            pltpu.VMEM((PLANES, ROWS, GROUP * HD), BF16),
            pltpu.VMEM((PLANES, GROUP * ROWS, 2 * HD), BF16),
            pltpu.VMEM((PLANES, ROWS, GROUP * HD), BF16),
            pltpu.VMEM((ROWS, CH), BF16),
            pltpu.VMEM((1, CH), F32),
            pltpu.VMEM((RING, 1, OWN), F32),
            pltpu.VMEM((NS, CH), F32),
            pltpu.VMEM((RING, NS, OWN), F32),
            pltpu.VMEM((NS + 8, OWN), F32),
            pltpu.VMEM((PLANES, NS + 8, OWN), F32),
            pltpu.VMEM((NS, OWN), F32),
            pltpu.VMEM((RING, NS, OWN), BF16),
            pltpu.VMEM((NS, CH), BF16),
            pltpu.VMEM((RING, NS + 8, OWN), F32),
            dma((3,)), dma((2,)), dma((4, 3)), dma((4, 3)),
            dma((5, 4)), dma((5, 4)), dma((5, 4)), dma((5, 4)), dma((ZN, 4)), dma((ZN, 4)),
            dma((RING,)), dma((RING,)), dma((RING,)), dma((RING,)), dma((PLANES,)), dma((PLANES,)), dma((RING,)), dma((RING,)),
            dma((PLANES,)), dma((PLANES,)), dma((4,)), dma((STORES,)),
        ],
        compiler_params=pltpu.CompilerParams(
            collective_id=0, has_side_effects=True, vmem_limit_bytes=60 * 2**20
        ),
        name="mixer",
    )(
        mamba_input, gate_branch, step_size, decay_rates.T, input_map.T, output_map.T, mixing_weight,
        mixing_bias.reshape(CH // 128, 128), skip_gain.reshape(1, CH), segments.reshape(PLANES * RING, ROWS),
        query_rows, key_rows, value_rows,
    )
    shapes = (jax.ShapeDtypeStruct(mixed.shape, BF16), jax.ShapeDtypeStruct(attended.shape, BF16))
    return pl.pallas_call(
        hand_over,
        out_shape=shapes,
        in_specs=[hbm] * 2,
        out_specs=(hbm, hbm),
        scratch_shapes=[
            pltpu.VMEM(mixed.shape, BF16), pltpu.VMEM(attended.shape, BF16), dma((2, 6)),
        ],
        compiler_params=pltpu.CompilerParams(vmem_limit_bytes=60 * 2**20),
        name="hand_over",
    )(mixed, attended)


def solution(mesh):
    split = P(("dp", "ctx"), None)
    in_specs = (
        split, split, split, P("dp", None), split, split, P(), P(), P(), P("dp"), split, split, split,
    )
    return jax.shard_map(
        on_device, mesh=mesh, in_specs=in_specs, out_specs=(split, split), check_vma=False
    )
```
